256 devices in a mesh: date: 64 (over x, z_lo, y), strip: 4 (over z_hi, core).
Axes of the slice: x: 4, y: 4, z: 8 (z_hi: 2, z_lo: 4; z = z_hi * 4 + z_lo), core: 2. Of those that a mesh axis runs over, the one named last changes fastest.
Arguments:
- slc: bfloat16 [2, 256, 512, 2048], P(None, 'date', 'strip'), may hold values from -40 to 40, as said below
- partner_offset: int32 [256, 4], P('date'), may hold values from -4 to 4, as said below
Outputs:
- interferogram: float32 [256, 4, 2, 128, 128], P('date', None, None, 'strip')
- coherence: float32 [256, 4, 128, 128], P('date', None, 'strip')
The draws below stay inside these ranges and needn't reach their ends.
Inputs may be any that keep to these rules, and one draw needn't show every extreme that they name: `slc`: complex samples as real and imaginary parts. `partner_offset`: each date's 4 offsets are nonzero and of distinct magnitudes, and date + offset lies in 0 to 255.
All inputs are finite; a program needn't handle non-finite values.
Results may differ from the reference program's by a relative error of at most 0.0003.
Values may be sent and summed in bfloat16 or wider, within the bound.
A program may use at most 128 MiB of HBM per device.

```python
import jax
import jax.numpy as jnp
from jax import lax

PARTNERS = 4
MAXOFF = 4
LOOK_AZ = 4
LOOK_RG = 16
RG = 2048
DATES = 256
AZ = 512


def draw_slc(key, part):
    key = jax.random.fold_in(key, 11)
    key_list = jax.random.split(key, 7)
    noise_field = jnp.clip(jax.random.normal(key_list[0], (2, DATES, AZ, RG), jnp.float32), -5.0, 5.0)
    common = jnp.clip(jax.random.normal(key_list[1], (2, AZ, RG), jnp.float32), -5.0, 5.0)
    height = jax.random.normal(key_list[2], (AZ, RG), jnp.float32)
    date_slope = jax.random.uniform(key_list[3], (DATES, 1, 1), jnp.float32, -1.5, 1.5)
    coherent_share = jax.random.uniform(key_list[4], (DATES, 1, 1), jnp.float32, 0.15, 0.9)
    row_amp = 10.0 ** (0.5 * jax.random.uniform(key_list[5], (AZ, 1), jnp.float32))
    col_amp = 10.0 ** (0.5 * jax.random.uniform(key_list[6], (1, RG), jnp.float32))
    amplitude = 0.3 * row_amp * col_amp
    phase_angle = height[None] * date_slope
    cosine = jnp.cos(phase_angle)
    sine_part = jnp.sin(phase_angle)
    turned_real = common[0][None] * cosine - common[1][None] * sine_part
    turned_imag = common[0][None] * sine_part + common[1][None] * cosine
    keep_share = jnp.sqrt(coherent_share)
    lose_share = jnp.sqrt(1.0 - coherent_share)
    real_part = amplitude * (keep_share * turned_real + lose_share * noise_field[0])
    imag_part = amplitude * (keep_share * turned_imag + lose_share * noise_field[1])
    return jnp.stack([real_part, imag_part]).astype(jnp.bfloat16)


def draw_partner_offset(key, part):
    key = jax.random.fold_in(key, 23)
    key_list = jax.random.split(key, 3)
    date_column = jnp.arange(DATES, dtype=jnp.int32)[:, None]
    first_step = jax.random.randint(key_list[0], (DATES, 1), 0, MAXOFF, jnp.int32)
    first_step = jnp.where((date_column == 0) | (date_column == DATES - 1), MAXOFF - 1, first_step)
    stride = 2 * jax.random.randint(key_list[1], (DATES, 1), 0, MAXOFF // 2, jnp.int32) + 1
    slot_index = jnp.arange(PARTNERS, dtype=jnp.int32)[None, :]
    magnitude = (first_step + slot_index * stride) % MAXOFF + 1
    heading = 2 * jax.random.randint(key_list[2], (DATES, PARTNERS), 0, 2, jnp.int32) - 1
    offset = heading * magnitude
    target = date_column + offset
    offset = jnp.where((target < 0) | (target >= DATES), -offset, offset)
    return offset.astype(jnp.int32)


def setup_inputs(seed: int = 0) -> dict:
    key_of = jax.random.split(jax.random.key(seed), 3)
    return {
        "slc": draw_slc(jax.random.fold_in(key_of[2], 71), 0),
        "partner_offset": draw_partner_offset(jax.random.fold_in(key_of[2], 71), 0),
    }


EPS = 1e-06

def range_sum(values):
    return values.reshape(values.shape[:-1] + (values.shape[-1] // LOOK_RG, LOOK_RG)).sum(-1)

def look_sums(own_tile, partner_tile):
    own_real = own_tile[0].astype(jnp.float32)[..., None, :, :]
    own_imag = own_tile[1].astype(jnp.float32)[..., None, :, :]
    far_real = partner_tile[0].astype(jnp.float32)
    far_imag = partner_tile[1].astype(jnp.float32)
    prod_real = range_sum(own_real * far_real + own_imag * far_imag)
    prod_imag = range_sum(own_imag * far_real - own_real * far_imag)
    own_power = jnp.broadcast_to(range_sum(own_real * own_real + own_imag * own_imag), prod_real.shape)
    far_power = range_sum(far_real * far_real + far_imag * far_imag)
    return jnp.stack([prod_real, prod_imag, own_power, far_power], axis=-3)

def finish(extended):
    margin = LOOK_AZ // 2
    total_rows = extended.shape[-2]
    columns = extended.shape[-1]
    inner_rows = extended[..., margin:total_rows - margin, :]
    leading = inner_rows.shape[:-2]
    looks = inner_rows.reshape(leading + (inner_rows.shape[-2] // LOOK_AZ, LOOK_AZ, columns)).sum(-2)
    interferogram = looks[..., 0:2, :, :] / float(LOOK_AZ * LOOK_RG)
    blocks = extended.reshape(leading + (total_rows // LOOK_AZ, LOOK_AZ, columns)).sum(-2)
    windows = blocks[..., :-1, :] + blocks[..., 1:, :]
    magnitude = jnp.sqrt(windows[..., 0, :, :] * windows[..., 0, :, :] + windows[..., 1, :, :] * windows[..., 1, :, :])
    coherence = magnitude / jnp.sqrt(windows[..., 2, :, :] * windows[..., 3, :, :] + EPS)
    return (interferogram, coherence)

def reference(slc, partner_offset):
    margin = LOOK_AZ // 2

    def one_date(date_index):
        own_tile = lax.dynamic_index_in_dim(slc, date_index, 1, keepdims=False)
        partner_dates = (date_index + partner_offset[date_index]).astype(jnp.int32)
        partner_tile = jnp.take(slc, partner_dates, axis=1)
        sums = look_sums(own_tile, partner_tile)
        padded = jnp.pad(sums, ((0, 0), (0, 0), (margin, margin), (0, 0)))
        return finish(padded)
    interferogram, coherence = lax.map(one_date, jnp.arange(DATES, dtype=jnp.int32))
    return (interferogram, coherence)
```

```python
import functools

import jax
import jax.numpy as jnp
from jax import lax
from jax.experimental import pallas as pl
from jax.experimental.pallas import tpu as pltpu
from jax.sharding import PartitionSpec as P

MESH = pl.DeviceIdType.MESH
OWN = 4
MAXOFF = 4
LOOK_AZ = 4
LOOK_RG = 16
EPS = 1e-06
STEP = 16
LANES = 256
PAD = 8
BLOCK = 8
IN_FLIGHT = 3

INNER = [(a, m) for a in range(4, 8) for m in range(1, 5) if a + m < 8]
CROSS = [(a, m) for a in (2, 3) for m in range(1, 5) if 4 <= a + m < 8]
CROSS += [(a, m) for a in range(4, 8) for m in range(1, 5) if a + m in (8, 9)]
FAR = [2, 3, 8, 9]


def slot(a, m):
    return 4 * a + m - 1


PLACE = {}
POWER = {}
for _edge in INNER:
    PLACE[_edge] = 2 * len(PLACE)
for _date in range(4, 8):
    POWER[_date] = 2 * len(INNER) + _date - 4
N_INNER = 2 * len(INNER) + 4
for _n, _edge in enumerate(CROSS):
    PLACE[_edge] = N_INNER + 2 * _n
for _n, _date in enumerate(FAR):
    POWER[_date] = N_INNER + 2 * len(CROSS) + _n
N_ALL = N_INNER + 2 * len(CROSS) + 4


def kernel(
    offsets, slc, interferogram, coherence,
    own, far, sel, sums, edge_sums, halo, results,
    own_sem, send_sem, recv_sem, halo_send, halo_recv, ship_send, ship_recv,
):
    rows = own.shape[2]
    cells = own.shape[3]
    steps = rows // STEP
    looks = rows // LOOK_AZ
    blocks = looks // BLOCK
    columns = cells // LOOK_RG
    d = lax.axis_index("date")
    s = lax.axis_index("strip")
    has = {
        "prev": d > 0,
        "next": d < lax.axis_size("date") - 1,
        "low": s > 0,
        "high": s < lax.axis_size("strip") - 1,
    }
    where = {
        "prev": {"date": d - 1},
        "next": {"date": d + 1},
        "low": {"strip": s - 1},
        "high": {"strip": s + 1},
    }
    order = [0, steps - 1] + list(range(1, steps - 1))

    def own_copy(step):
        part = (slice(None), slice(None), pl.ds(step * STEP, STEP))
        return pltpu.make_async_copy(slc.at[part], own.at[part], own_sem.at[step])

    def image_copy(side, step):
        n = 0 if side == "next" else 1
        first = 2 if side == "next" else 0
        return pltpu.make_async_remote_copy(
            src_ref=slc.at[:, pl.ds(first, 2), pl.ds(step * STEP, STEP)],
            dst_ref=far.at[n, :, :, pl.ds(step * STEP, STEP)],
            send_sem=send_sem.at[n, step],
            recv_sem=recv_sem.at[n, step],
            device_id=where[side],
            device_id_type=MESH,
        )

    def halo_copy(side):
        n = 0 if side == "high" else 1
        return pltpu.make_async_remote_copy(
            src_ref=edge_sums.at[n],
            dst_ref=halo.at[n],
            send_sem=halo_send.at[n],
            recv_sem=halo_recv.at[n],
            device_id=where[side],
            device_id_type=MESH,
        )

    def ship_copies(side, block):
        n, base, shift = (0, 16, -16) if side == "next" else (1, 8, 16)
        part = pl.ds(block * BLOCK, BLOCK)
        copies = []
        for i, (first, count) in enumerate(((3, 1), (6, 2))):
            copies.append(
                pltpu.make_async_remote_copy(
                    src_ref=results.at[pl.ds(base + first, count), :, part],
                    dst_ref=results.at[pl.ds(base + shift + first, count), :, part],
                    send_sem=ship_send.at[n, block, i],
                    recv_sem=ship_recv.at[n, block, i],
                    device_id=where[side],
                    device_id_type=MESH,
                )
            )
        return copies

    for step in order:
        own_copy(step).start()

    barrier = pltpu.get_barrier_semaphore()
    for side in has:
        @pl.when(has[side])
        def _(side=side):
            pl.semaphore_signal(barrier, inc=1, device_id=where[side], device_id_type=MESH)

    cell = lax.broadcasted_iota(jnp.int32, (cells, columns), 0)
    look = lax.broadcasted_iota(jnp.int32, (cells, columns), 1)
    sel[...] = jnp.where(cell // LOOK_RG == look, 1.0, 0.0).astype(jnp.bfloat16)

    pl.semaphore_wait(barrier, sum(h.astype(jnp.int32) for h in has.values()))

    def send(step):
        for side in ("next", "prev"):
            @pl.when(has[side])
            def _(side=side):
                image_copy(side, step).start()

    for step in order[:IN_FLIGHT]:
        send(step)

    for side, n in (("prev", 0), ("next", 1)):
        @pl.when(jnp.logical_not(has[side]))
        def _(n=n, side=side):
            far[n] = jnp.zeros(far.shape[1:], far.dtype)
            base = 3 if side == "prev" else 27
            results[base] = jnp.zeros(results.shape[1:], results.dtype)
            results[pl.ds(base + 3, 2)] = jnp.zeros((2,) + results.shape[1:], results.dtype)
    for side, n in (("low", 0), ("high", 1)):
        @pl.when(jnp.logical_not(has[side]))
        def _(n=n):
            halo[n] = jnp.zeros(halo.shape[1:], halo.dtype)

    def add_up(step, edges, dates, first, count):
        row = pl.ds(step * STEP, STEP)
        needed = sorted({a for a, m in edges} | {a + m for a, m in edges} | set(dates))

        def body(k, total):
            lane = pl.ds(pl.multiple_of(k * LANES, LANES), LANES)
            value = {}
            for a in needed:
                if 4 <= a < 8:
                    parts = [own[c, a - 4, row, lane] for c in range(2)]
                elif a < 4:
                    parts = [far[0, c, a - 2, row, lane] for c in range(2)]
                else:
                    parts = [far[1, c, a - 8, row, lane] for c in range(2)]
                value[a] = [p.astype(jnp.float32) for p in parts]
            terms = []
            for a, m in edges:
                (x, y), (u, v) = value[a], value[a + m]
                terms.append(x * u + y * v)
                terms.append(y * u - x * v)
            for a in dates:
                x, y = value[a]
                terms.append(x * x + y * y)
            packed = []
            for t in terms:
                high = t.astype(jnp.bfloat16)
                low = (t - high.astype(jnp.float32)).astype(jnp.bfloat16)
                packed.append(jnp.concatenate([high, low], axis=1))
            left = jnp.concatenate(packed, axis=0)
            weight = sel[lane, :]
            right = jnp.concatenate([weight, weight], axis=0)
            return total + jnp.dot(left, right, preferred_element_type=jnp.float32)

        total = lax.fori_loop(0, cells // LANES, body, jnp.zeros((count * STEP, columns), jnp.float32))
        sums[pl.ds(first, count), pl.ds(PAD + step * STEP, STEP), :] = total.reshape(count, STEP, columns)

    def windows(q, block):
        base = PAD + block * BLOCK * LOOK_AZ

        def every(shift):
            return sums[q, pl.ds(base + shift, BLOCK, stride=LOOK_AZ), :]

        inner = (every(0) + every(1)) + (every(2) + every(3))
        outer = (every(-2) + every(-1)) + (every(4) + every(5))
        return inner, inner + outer

    def finish(block, edges, power):
        for a, m in edges:
            for b in (a, a + m):
                if b not in power:
                    power[b] = windows(POWER[b], block)[1]
            look_re, win_re = windows(PLACE[a, m], block)
            look_im, win_im = windows(PLACE[a, m] + 1, block)
            size = jnp.sqrt(win_re * win_re + win_im * win_im)
            part = pl.ds(block * BLOCK, BLOCK)
            results[slot(a, m), 0, part] = look_re * (1.0 / (LOOK_AZ * LOOK_RG))
            results[slot(a, m), 1, part] = look_im * (1.0 / (LOOK_AZ * LOOK_RG))
            results[slot(a, m), 2, part] = size / jnp.sqrt(power[a] * power[a + m] + EPS)

    for step in order:
        own_copy(step).wait()
        add_up(step, INNER, list(range(4, 8)), 0, N_INNER)

    shipped = [(4, 4), (5, 3), (5, 4), (2, 4), (3, 3), (3, 4)]
    kept = INNER + [e for e in CROSS if e not in shipped]

    def finish_block(block):
        power = {}
        finish(block, shipped, power)
        for side in ("next", "prev"):
            @pl.when(has[side])
            def _(side=side):
                for copy in ship_copies(side, block):
                    copy.start()
        finish(block, kept, power)

    ready = set()
    finished = set()
    for n, step in enumerate(order):
        for side in ("prev", "next"):
            @pl.when(has[side])
            def _(side=side):
                image_copy("next" if side == "prev" else "prev", step).wait_recv()
        if n + IN_FLIGHT < steps:
            send(order[n + IN_FLIGHT])
        add_up(step, CROSS, FAR, N_INNER, N_ALL - N_INNER)
        ready.add(step)
        if n == 1:
            for q in range(N_ALL):
                edge_sums[0, pl.ds(q, 1)] = sums[q, pl.ds(PAD + rows - 2, 1)] + sums[q, pl.ds(PAD + rows - 1, 1)]
                edge_sums[1, pl.ds(q, 1)] = sums[q, pl.ds(PAD, 1)] + sums[q, pl.ds(PAD + 1, 1)]
            for side in ("high", "low"):
                @pl.when(has[side])
                def _(side=side):
                    halo_copy(side).start()
        if n == 2:
            for side, opposite in (("low", "high"), ("high", "low")):
                @pl.when(has[side])
                def _(opposite=opposite):
                    halo_copy(opposite).wait_recv()
            zero = jnp.zeros((1, columns), jnp.float32)
            for q in range(N_ALL):
                sums[q, pl.ds(PAD - 2, 1)] = zero
                sums[q, pl.ds(PAD - 1, 1)] = halo[0, pl.ds(q, 1)]
                sums[q, pl.ds(PAD + rows, 1)] = halo[1, pl.ds(q, 1)]
                sums[q, pl.ds(PAD + rows + 1, 1)] = zero
        if n >= 2:
            per = BLOCK * LOOK_AZ // STEP
            for block in range(blocks):
                touched = {p for p in range(block * per - 1, block * per + per + 1) if 0 <= p < steps}
                if block not in finished and touched <= ready:
                    finish_block(block)
                    finished.add(block)

    for side, opposite in (("next", "prev"), ("prev", "next")):
        @pl.when(has[side])
        def _(side=side, opposite=opposite):
            for block in range(blocks):
                for copy in ship_copies(opposite, block):
                    copy.wait_recv()

    for i in range(OWN):
        for k in range(4):
            offset = offsets[i, k]
            place = 4 * (OWN + i + jnp.minimum(offset, 0)) + jnp.abs(offset) - 1
            sign = jnp.where(offset > 0, 1.0, -1.0)
            chosen = results[place]
            interferogram[i, k, 0] = chosen[0]
            interferogram[i, k, 1] = chosen[1] * sign
            coherence[i, k] = chosen[2]

    for side in ("next", "prev"):
        @pl.when(has[side])
        def _(side=side):
            for step in order:
                image_copy(side, step).wait_send()
            for block in range(blocks):
                for copy in ship_copies(side, block):
                    copy.wait_send()
    for side in ("high", "low"):
        @pl.when(has[side])
        def _(side=side):
            halo_copy(side).wait_send()


def per_device(slc, partner_offset):
    _, dates, rows, cells = slc.shape
    columns = cells // LOOK_RG
    looks = rows // LOOK_AZ
    steps = rows // STEP
    blocks = looks // BLOCK
    f32 = jnp.float32
    return pl.pallas_call(
        kernel,
        out_shape=(
            jax.ShapeDtypeStruct((dates, 4, 2, looks, columns), f32),
            jax.ShapeDtypeStruct((dates, 4, looks, columns), f32),
        ),
        in_specs=[
            pl.BlockSpec(memory_space=pltpu.SMEM),
            pl.BlockSpec(memory_space=pl.ANY),
        ],
        out_specs=[pl.BlockSpec(memory_space=pltpu.VMEM)] * 2,
        scratch_shapes=[
            pltpu.VMEM((2, dates, rows, cells), slc.dtype),
            pltpu.VMEM((2, 2, 2, rows, cells), slc.dtype),
            pltpu.VMEM((cells, columns), jnp.bfloat16),
            pltpu.VMEM((N_ALL, rows + 2 * PAD, columns), f32),
            pltpu.VMEM((2, N_ALL, columns), f32),
            pltpu.VMEM((2, N_ALL, columns), f32),
            pltpu.VMEM((32, 3, looks, columns), f32),
            pltpu.SemaphoreType.DMA((steps,)),
            pltpu.SemaphoreType.DMA((2, steps)),
            pltpu.SemaphoreType.DMA((2, steps)),
            pltpu.SemaphoreType.DMA((2,)),
            pltpu.SemaphoreType.DMA((2,)),
            pltpu.SemaphoreType.DMA((2, blocks, 2)),
            pltpu.SemaphoreType.DMA((2, blocks, 2)),
        ],
        compiler_params=pltpu.CompilerParams(
            collective_id=0, has_side_effects=True, vmem_limit_bytes=48 * 1024 * 1024
        ),
    )(partner_offset, slc)


def solution(mesh):
    return jax.shard_map(
        per_device,
        mesh=mesh,
        in_specs=(P(None, "date", "strip", None), P("date", None)),
        out_specs=(P("date", None, None, "strip", None), P("date", None, "strip", None)),
        check_vma=False,
    )
```

```python
import functools

import jax
import jax.numpy as jnp
from jax import lax
from jax.experimental import pallas as pl
from jax.experimental.pallas import tpu as pltpu
from jax.sharding import PartitionSpec as P

MESH = pl.DeviceIdType.MESH
OWN = 4
MAXOFF = 4
LOOK_AZ = 4
LOOK_RG = 16
EPS = 1e-06
LANES = 1024
INNER_ROWS = 32
PAD = 8
BLOCK = 8
IN_FLIGHT = 3
BOTH, NEAR, OTHER = (0, 2), (0, 1), (1, 2)
UNITS = [(0, 16, BOTH), (112, 16, BOTH)]
UNITS += [(16, 32, NEAR), (48, 32, NEAR), (80, 32, NEAR)]
UNITS += [(80, 32, OTHER), (48, 32, OTHER), (32, 16, OTHER), (16, 16, OTHER)]
EDGES_AT = 1
RELAY_AT = (2, 4)
HALO_AT = 7

INNER = [(a, m) for a in range(4, 8) for m in range(1, 5) if a + m < 8]
CROSS = {
    NEAR: [(3, m) for m in range(1, 5)] + [(a, 8 - a) for a in range(4, 8)],
    OTHER: [(2, m) for m in range(2, 5)] + [(a, 9 - a) for a in range(5, 8)],
}
FAR = {NEAR: [3, 8], OTHER: [2, 9]}


def slot(a, m):
    return 4 * a + m - 1


PLACE = {}
POWER = {}
SPAN = {}


def give_places(name, edges, dates):
    first = 2 * len(PLACE) + len(POWER)
    for edge in edges:
        PLACE[edge] = 2 * len(PLACE) + len(POWER)
    for date in dates:
        POWER[date] = 2 * len(PLACE) + len(POWER)
    SPAN[name] = (first, 2 * len(PLACE) + len(POWER) - first)


give_places("inner", INNER, [4, 5, 6, 7])
give_places(NEAR, CROSS[NEAR], FAR[NEAR])
give_places(OTHER, CROSS[OTHER], FAR[OTHER])
N_ALL = SPAN[OTHER][0] + SPAN[OTHER][1]
SHIPPED = {"next": [(4, 4), (5, 3), (5, 4)], "prev": [(3, 3), (3, 4), (2, 4)]}


def kernel(
    offsets, slc, interferogram, coherence,
    own, far, own_wide, far_wide, sel, sums, edge_sums, halo, relayed, results,
    own_sem, send_sem, recv_sem, halo_send, halo_recv, relay_send, relay_recv, ship_send, ship_recv,
):
    rows = own.shape[2]
    cells = own.shape[3]
    looks = rows // LOOK_AZ
    blocks = looks // BLOCK
    columns = cells // LOOK_RG
    d = lax.axis_index("date")
    s = lax.axis_index("strip")
    has = {
        "prev": d > 0,
        "next": d < lax.axis_size("date") - 1,
        "low": s > 0,
        "high": s < lax.axis_size("strip") - 1,
    }
    where = {
        "prev": {"date": d - 1},
        "next": {"date": d + 1},
        "low": {"strip": s - 1},
        "high": {"strip": s + 1},
    }
    place = d % 4
    inner = (place == 1) | (place == 2)
    remote = {"high": s % 2 == 1, "low": s % 2 == 0}
    greets = {
        "prev": has["prev"],
        "next": has["next"],
        "low": has["low"] & (inner | jnp.logical_not(remote["low"])),
        "high": has["high"] & (inner | jnp.logical_not(remote["high"])),
    }
    false = d < 0
    later = {"prev": false, "next": false, "low": false, "high": remote["high"]}
    former = {"prev": false, "next": false, "low": remote["low"], "high": false}

    def own_copy(step):
        part = (slice(None), slice(None), pl.ds(step * INNER_ROWS, INNER_ROWS))
        return pltpu.make_async_copy(slc.at[part], own.at[part], own_sem.at[step])

    def image_copy(side, unit):
        first, height, (low, high) = UNITS[unit]
        n = 0 if side == "next" else 1
        row = pl.ds(first, height)
        date = pl.ds(4 - high, high - low) if side == "next" else pl.ds(low, high - low)
        slots = pl.ds(2 - high, high - low) if side == "next" else pl.ds(low, high - low)
        return pltpu.make_async_remote_copy(
            src_ref=slc.at[:, date, row],
            dst_ref=far.at[n, :, slots, row],
            send_sem=send_sem.at[n, unit],
            recv_sem=recv_sem.at[n, unit],
            device_id=where[side],
            device_id_type=MESH,
        )

    def halo_copy(n, source, side, send, target=None, recv=None):
        return pltpu.make_async_remote_copy(
            src_ref=source,
            dst_ref=halo.at[n] if target is None else target,
            send_sem=send,
            recv_sem=halo_recv.at[n] if recv is None else recv,
            device_id=where[side],
            device_id_type=MESH,
        )

    def ship_copy(side, edge, block):
        a, m = edge
        n, shift = (0, -16) if side == "next" else (1, 16)
        i = SHIPPED[side].index(edge)
        part = pl.ds(block * BLOCK, BLOCK)
        return pltpu.make_async_remote_copy(
            src_ref=results.at[slot(a, m), :, part],
            dst_ref=results.at[slot(a, m) + shift, :, part],
            send_sem=ship_send.at[n, i, block],
            recv_sem=ship_recv.at[n, i, block],
            device_id=where[side],
            device_id_type=MESH,
        )

    for step in range(rows // INNER_ROWS):
        own_copy(step).start()

    barrier = pltpu.get_barrier_semaphore()

    def count(flags):
        return sum(flag.astype(jnp.int32) for flag in flags)

    for side in has:
        @pl.when(greets[side] & jnp.logical_not(later[side] | former[side]))
        def _(side=side):
            pl.semaphore_signal(barrier, inc=1, device_id=where[side], device_id_type=MESH)

    look = lax.broadcasted_iota(jnp.int32, (128, columns), 1)
    cell = lax.broadcasted_iota(jnp.int32, (128, columns), 0)
    for tile in range(cells // 128):
        ones = jnp.where((cell + tile * 128) // LOOK_RG == look, 1.0, 0.0).astype(jnp.bfloat16)
        sel[tile, pl.ds(0, 128)] = ones
        sel[tile, pl.ds(128, 128)] = ones

    pl.semaphore_wait(barrier, count(greets[side] & jnp.logical_not(later[side]) for side in has))
    for side in has:
        @pl.when(greets[side] & (later[side] | former[side]))
        def _(side=side):
            pl.semaphore_signal(barrier, inc=1, device_id=where[side], device_id_type=MESH)

    def send(unit):
        for side in ("next", "prev"):
            @pl.when(has[side])
            def _(side=side):
                image_copy(side, unit).start()

    for unit in range(IN_FLIGHT):
        send(unit)

    for side, n in (("prev", 0), ("next", 1)):
        @pl.when(jnp.logical_not(has[side]))
        def _(n=n, side=side):
            far[n] = jnp.zeros(far.shape[1:], far.dtype)
            base = 3 if side == "prev" else 27
            results[base] = jnp.zeros(results.shape[1:], results.dtype)
            results[pl.ds(base + 3, 2)] = jnp.zeros((2,) + results.shape[1:], results.dtype)
    for side, n in (("low", 0), ("high", 1)):
        @pl.when(jnp.logical_not(has[side]))
        def _(n=n):
            halo[n] = jnp.zeros(halo.shape[1:], halo.dtype)

    def widen(source, target, row):
        def body(k, carry):
            lane = pl.ds(pl.multiple_of(k * 128, 128), 128)
            target[:, :, k] = source[:, :, row, lane].astype(jnp.float32)
            return carry

        lax.fori_loop(0, cells // 128, body, 0, unroll=2)

    def add_up(base, far_base, height, edges, dates, first, count):
        pairs = height // 2
        groups = edges if dates is None else [(edges, dates)]
        every = [e for pairs_of, _ in groups for e in pairs_of]
        needed = sorted({a for a, m in every} | {a + m for a, m in every})

        def body(k, total):
            packed = []
            weights = []
            for part in range(LANES // 128):
                tile = k * (LANES // 128) + part
                value = {}
                for a in needed:
                    value[a] = []
                    for c in range(2):
                        for odd in range(2):
                            row = pl.ds((base if 4 <= a < 8 else far_base) + odd, pairs, stride=2)
                            if 4 <= a < 8:
                                value[a].append(own_wide[c, a - 4, tile, row])
                            elif a < 4:
                                value[a].append(far_wide[0, c, a - 2, tile, row])
                            else:
                                value[a].append(far_wide[1, c, a - 8, tile, row])
                terms = []
                for pairs_of, alone in groups:
                    for a, m in pairs_of:
                        (x, z, y, w), (u, p, v, q) = value[a], value[a + m]
                        terms.append((x * u + y * v) + (z * p + w * q))
                        terms.append((y * u - x * v) + (w * p - z * q))
                    for a in alone:
                        x, z, y, w = value[a]
                        terms.append((x * x + y * y) + (z * z + w * w))
                left = jnp.concatenate(terms, axis=0)
                high = left.astype(jnp.bfloat16)
                low = (left - high.astype(jnp.float32)).astype(jnp.bfloat16)
                packed += [high, low]
                weights.append(sel[tile])
            left = jnp.concatenate(packed, axis=1)
            right = jnp.concatenate(weights, axis=0)
            return total + jnp.dot(left, right, preferred_element_type=jnp.float32)

        total = lax.fori_loop(0, cells // LANES, body, jnp.zeros((count * pairs, columns), jnp.float32))
        sums[pl.ds(first, count), pl.ds(PAD + base // 2, pairs), :] = total.reshape(count, pairs, columns)

    def windows(q, block):
        base = PAD + block * BLOCK * 2

        def every(shift):
            return sums[q, pl.ds(base + shift, BLOCK, stride=2), :]

        inner = every(0) + every(1)
        return inner, inner + (every(-1) + every(2))

    def finish(block, edges, power):
        for a, m in edges:
            for b in (a, a + m):
                if b not in power:
                    power[b] = windows(POWER[b], block)[1]
            look_re, win_re = windows(PLACE[a, m], block)
            look_im, win_im = windows(PLACE[a, m] + 1, block)
            size = jnp.sqrt(win_re * win_re + win_im * win_im)
            part = pl.ds(block * BLOCK, BLOCK)
            results[slot(a, m), 0, part] = look_re * (1.0 / (LOOK_AZ * LOOK_RG))
            results[slot(a, m), 1, part] = look_im * (1.0 / (LOOK_AZ * LOOK_RG))
            results[slot(a, m), 2, part] = size / jnp.sqrt(power[a] * power[a + m] + EPS)

    for step in range(rows // INNER_ROWS):
        own_copy(step).wait()
        row = pl.ds(step * INNER_ROWS, INNER_ROWS)
        widen(own, own_wide.at[:, :, :, row], row)
        add_up(step * INNER_ROWS, 0, INNER_ROWS, INNER, [4, 5, 6, 7], *SPAN["inner"])

    @pl.when(greets["high"] & later["high"])
    def _():
        pl.semaphore_wait(barrier, 1)

    def on_strip(which, body):
        for side, n in (("high", 0), ("low", 1)):
            @pl.when(has[side] & remote[side] & which)
            def _(side=side, n=n):
                body(side, n)

    def send_edges():
        for q in range(N_ALL):
            edge_sums[0, pl.ds(q, 1)] = sums[q, pl.ds(PAD + rows // 2 - 1, 1)]
            edge_sums[1, pl.ds(q, 1)] = sums[q, pl.ds(PAD, 1)]
        for side, n in (("high", 0), ("low", 1)):
            @pl.when(has[side] & jnp.logical_not(remote[side]))
            def _(side=side, n=n):
                halo_copy(n, edge_sums.at[n], side, halo_send.at[n]).start()
        on_strip(inner, lambda side, n: halo_copy(n, edge_sums.at[n], side, halo_send.at[n]).start())
        for at, toward in ((0, "next"), (3, "prev")):
            on_strip(place == at, lambda side, n, toward=toward: relay_out(n, toward).start())

    def relay_out(n, toward):
        return halo_copy(n, edge_sums.at[n], toward, relay_send.at[0], relayed.at[0], relay_recv.at[0])

    def relay_over(side, n):
        return halo_copy(n, relayed.at[0], side, relay_send.at[1], relayed.at[1], relay_recv.at[1])

    def relay_back(n, toward):
        return halo_copy(1 - n, relayed.at[1], toward, relay_send.at[2])

    def pass_over(side, n):
        relay_out(n, "next").wait_recv()
        relay_over(side, n).start()

    def pass_back():
        for at, toward in ((1, "prev"), (2, "next")):
            def body(side, n, toward=toward):
                relay_over(side, n).wait_recv()
                relay_back(n, toward).start()
            on_strip(place == at, body)

    def take_halo():
        for side, opposite, n in (("low", "high", 0), ("high", "low", 1)):
            @pl.when(has[side])
            def _(opposite=opposite, n=n):
                halo_copy(n, edge_sums.at[n], opposite, halo_send.at[n]).wait_recv()
        for q in range(N_ALL):
            sums[q, pl.ds(PAD - 1, 1)] = halo[0, pl.ds(q, 1)]
            sums[q, pl.ds(PAD + rows // 2, 1)] = halo[1, pl.ds(q, 1)]

    def finish_block(name, block):
        edges = INNER if name == "inner" else CROSS[name]
        power = {}
        for side in ("next", "prev"):
            owed = [e for e in edges if e in SHIPPED[side]]
            finish(block, owed, power)
            if owed:
                @pl.when(has[side])
                def _(side=side, owed=owed):
                    for edge in owed:
                        ship_copy(side, edge, block).start()
        finish(block, [e for e in edges if e not in SHIPPED["next"] + SHIPPED["prev"]], power)

    ready = {"inner": set(range(rows)), NEAR: set(), OTHER: set()}
    finished = set()
    for unit, (first, height, dates) in enumerate(UNITS):
        for side in ("prev", "next"):
            @pl.when(has[side])
            def _(side=side):
                image_copy("next" if side == "prev" else "prev", unit).wait_recv()
        if unit + IN_FLIGHT < len(UNITS):
            send(unit + IN_FLIGHT)
        if unit == HALO_AT:
            take_halo()
        row = pl.ds(first, height)
        for side, (low, high) in ((0, (2 - dates[1], 2 - dates[0])), (1, dates)):
            date = pl.ds(low, high - low)
            widen(far.at[side, :, date], far_wide.at[side, :, date, :, pl.ds(0, height)], row)
        names = [name for name in (NEAR, OTHER) if dates[0] <= name[0] and name[1] <= dates[1]]
        begin = SPAN[names[0]][0]
        number = sum(SPAN[name][1] for name in names)
        edges = [(CROSS[name], FAR[name]) for name in names]
        add_up(first, 0, height, edges, None, begin, number)
        for name in names:
            ready[name] |= set(range(first, first + height))
        if unit == EDGES_AT:
            send_edges()
        if unit == RELAY_AT[0]:
            on_strip(inner, pass_over)
        if unit == RELAY_AT[1]:
            pass_back()
        if unit > EDGES_AT:
            for name in (NEAR, OTHER, "inner"):
                for block in range(blocks):
                    height_of = BLOCK * LOOK_AZ
                    reach = set(range(max(block * height_of - 2, 0), min((block + 1) * height_of + 2, rows)))
                    inside = 0 < block < blocks - 1
                    if (name, block) not in finished and reach <= ready[name] and (inside or unit >= HALO_AT):
                        finish_block(name, block)
                        finished.add((name, block))

    for side, opposite in (("next", "prev"), ("prev", "next")):
        @pl.when(has[side])
        def _(side=side, opposite=opposite):
            for block in range(blocks):
                for edge in SHIPPED[opposite]:
                    ship_copy(opposite, edge, block).wait_recv()

    for i in range(OWN):
        for k in range(4):
            offset = offsets[i, k]
            place = 4 * (OWN + i + jnp.minimum(offset, 0)) + jnp.abs(offset) - 1
            sign = jnp.where(offset > 0, 1.0, -1.0)
            chosen = results[place]
            interferogram[i, k, 0] = chosen[0]
            interferogram[i, k, 1] = chosen[1] * sign
            coherence[i, k] = chosen[2]

    for side in ("next", "prev"):
        @pl.when(has[side])
        def _(side=side):
            for unit in range(len(UNITS)):
                image_copy(side, unit).wait_send()
            for block in range(blocks):
                for edge in SHIPPED[side]:
                    ship_copy(side, edge, block).wait_send()
    for side, n in (("high", 0), ("low", 1)):
        @pl.when(has[side] & (inner | jnp.logical_not(remote[side])))
        def _(side=side, n=n):
            halo_copy(n, edge_sums.at[n], side, halo_send.at[n]).wait_send()
    on_strip(jnp.logical_not(inner), lambda side, n: relay_out(n, "next").wait_send())
    on_strip(inner, lambda side, n: relay_over(side, n).wait_send())
    on_strip(inner, lambda side, n: relay_back(n, "next").wait_send())


def per_device(slc, partner_offset):
    _, dates, rows, cells = slc.shape
    columns = cells // LOOK_RG
    looks = rows // LOOK_AZ
    steps = rows // INNER_ROWS
    blocks = looks // BLOCK
    f32 = jnp.float32
    return pl.pallas_call(
        kernel,
        out_shape=(
            jax.ShapeDtypeStruct((dates, 4, 2, looks, columns), f32),
            jax.ShapeDtypeStruct((dates, 4, looks, columns), f32),
        ),
        in_specs=[
            pl.BlockSpec(memory_space=pltpu.SMEM),
            pl.BlockSpec(memory_space=pl.ANY),
        ],
        out_specs=[pl.BlockSpec(memory_space=pltpu.VMEM)] * 2,
        scratch_shapes=[
            pltpu.VMEM((2, dates, rows, cells), slc.dtype),
            pltpu.VMEM((2, 2, 2, rows, cells), slc.dtype),
            pltpu.VMEM((2, dates, cells // 128, rows, 128), f32),
            pltpu.VMEM((2, 2, 2, cells // 128, INNER_ROWS, 128), f32),
            pltpu.VMEM((cells // 128, 256, columns), jnp.bfloat16),
            pltpu.VMEM((N_ALL, rows // 2 + 2 * PAD, columns), f32),
            pltpu.VMEM((2, N_ALL, columns), f32),
            pltpu.VMEM((2, N_ALL, columns), f32),
            pltpu.VMEM((2, N_ALL, columns), f32),
            pltpu.VMEM((32, 3, looks, columns), f32),
            pltpu.SemaphoreType.DMA((steps,)),
            pltpu.SemaphoreType.DMA((2, len(UNITS))),
            pltpu.SemaphoreType.DMA((2, len(UNITS))),
            pltpu.SemaphoreType.DMA((2,)),
            pltpu.SemaphoreType.DMA((2,)),
            pltpu.SemaphoreType.DMA((3,)),
            pltpu.SemaphoreType.DMA((2,)),
            pltpu.SemaphoreType.DMA((2, 3, blocks)),
            pltpu.SemaphoreType.DMA((2, 3, blocks)),
        ],
        compiler_params=pltpu.CompilerParams(
            collective_id=0, has_side_effects=True, vmem_limit_bytes=59 * 1024 * 1024
        ),
    )(partner_offset, slc)


def solution(mesh):
    return jax.shard_map(
        per_device,
        mesh=mesh,
        in_specs=(P(None, "date", "strip", None), P("date", None)),
        out_specs=(P("date", None, None, "strip", None), P("date", None, "strip", None)),
        check_vma=False,
    )
```

```python
import functools

import jax
import jax.numpy as jnp
from jax import lax
from jax.experimental import pallas as pl
from jax.experimental.pallas import tpu as pltpu
from jax.sharding import PartitionSpec as P

MESH = pl.DeviceIdType.MESH
OWN = 4
MAXOFF = 4
LOOK_AZ = 4
LOOK_RG = 16
EPS = 1e-06
LANES = 1024
INNER_ROWS = 32
PAD = 8
BLOCK = 8
IN_FLIGHT = 3
BOTH, NEAR, OTHER = (0, 2), (0, 1), (1, 2)
UNITS = [(0, 16, BOTH), (112, 16, BOTH)]
UNITS += [(16, 32, NEAR), (48, 32, NEAR), (80, 32, NEAR)]
UNITS += [(80, 32, OTHER), (48, 32, OTHER), (32, 16, OTHER), (16, 16, OTHER)]
EDGES_AT = 1
RELAY_AT = (2, 4)
SHIP_AT = 6
HALO_AT = 7

INNER = [(a, m) for a in range(4, 8) for m in range(1, 5) if a + m < 8]
CROSS = {
    NEAR: [(3, m) for m in range(1, 5)] + [(a, 8 - a) for a in range(4, 8)],
    OTHER: [(2, m) for m in range(2, 5)] + [(a, 9 - a) for a in range(5, 8)],
}
FAR = {NEAR: [3, 8], OTHER: [2, 9]}


def slot(a, m):
    return 4 * a + m - 1


PLACE = {}
POWER = {}
SPAN = {}


def give_places(name, edges, dates):
    first = 2 * len(PLACE) + len(POWER)
    for edge in edges:
        PLACE[edge] = 2 * len(PLACE) + len(POWER)
    for date in dates:
        POWER[date] = 2 * len(PLACE) + len(POWER)
    SPAN[name] = (first, 2 * len(PLACE) + len(POWER) - first)


give_places("inner", INNER, [4, 5, 6, 7])
give_places(NEAR, CROSS[NEAR], FAR[NEAR])
give_places(OTHER, CROSS[OTHER], FAR[OTHER])
N_ALL = SPAN[OTHER][0] + SPAN[OTHER][1]
SHIPPED = {"next": [(4, 4), (5, 3), (5, 4)], "prev": [(3, 3), (3, 4), (2, 4)]}


def kernel(
    partner_offset, slc, interferogram, coherence,
    offsets, own, far, own_wide, far_wide, sel, sums, edge_sums, halo, relayed, results,
    offset_sem, own_sem, send_sem, recv_sem, halo_send, halo_recv, relay_send, relay_recv, ship_send, ship_recv,
):
    rows = own.shape[2]
    cells = own.shape[3]
    looks = rows // LOOK_AZ
    blocks = looks // BLOCK
    columns = cells // LOOK_RG
    d = lax.axis_index("date")
    s = lax.axis_index("strip")
    has = {
        "prev": d > 0,
        "next": d < lax.axis_size("date") - 1,
        "low": s > 0,
        "high": s < lax.axis_size("strip") - 1,
    }
    where = {
        "prev": {"date": d - 1},
        "next": {"date": d + 1},
        "low": {"strip": s - 1},
        "high": {"strip": s + 1},
    }
    place = d % 4
    inner = (place == 1) | (place == 2)
    remote = {"high": s % 2 == 1, "low": s % 2 == 0}
    greets = {
        "prev": has["prev"],
        "next": has["next"],
        "low": has["low"] & (inner | jnp.logical_not(remote["low"])),
        "high": has["high"] & (inner | jnp.logical_not(remote["high"])),
    }
    false = d < 0
    later = {"prev": false, "next": false, "low": false, "high": remote["high"]}
    former = {"prev": false, "next": false, "low": remote["low"], "high": false}

    def own_copy(step):
        part = (slice(None), slice(None), pl.ds(step * INNER_ROWS, INNER_ROWS))
        return pltpu.make_async_copy(slc.at[part], own.at[part], own_sem.at[step])

    def image_copy(side, unit):
        first, height, (low, high) = UNITS[unit]
        n = 0 if side == "next" else 1
        row = pl.ds(first, height)
        date = pl.ds(4 - high, high - low) if side == "next" else pl.ds(low, high - low)
        slots = pl.ds(2 - high, high - low) if side == "next" else pl.ds(low, high - low)
        return pltpu.make_async_remote_copy(
            src_ref=slc.at[:, date, row],
            dst_ref=far.at[n, :, slots, row],
            send_sem=send_sem.at[n, unit],
            recv_sem=recv_sem.at[n, unit],
            device_id=where[side],
            device_id_type=MESH,
        )

    def halo_copy(n, source, side, send, target=None, recv=None):
        return pltpu.make_async_remote_copy(
            src_ref=source,
            dst_ref=halo.at[n] if target is None else target,
            send_sem=send,
            recv_sem=halo_recv.at[n] if recv is None else recv,
            device_id=where[side],
            device_id_type=MESH,
        )

    def ship_copy(side, edge, block):
        a, m = edge
        n, shift = (0, -16) if side == "next" else (1, 16)
        i = SHIPPED[side].index(edge)
        part = pl.ds(block * BLOCK, BLOCK)
        return pltpu.make_async_remote_copy(
            src_ref=results.at[slot(a, m), :, part],
            dst_ref=results.at[slot(a, m) + shift, :, part],
            send_sem=ship_send.at[n, i, block],
            recv_sem=ship_recv.at[n, i, block],
            device_id=where[side],
            device_id_type=MESH,
        )

    offset_copy = pltpu.make_async_copy(partner_offset, offsets, offset_sem)
    for step in range(rows // INNER_ROWS):
        own_copy(step).start()
    offset_copy.start()

    barrier = pltpu.get_barrier_semaphore()

    def count(flags):
        return sum(flag.astype(jnp.int32) for flag in flags)

    for side in has:
        @pl.when(greets[side] & jnp.logical_not(later[side] | former[side]))
        def _(side=side):
            pl.semaphore_signal(barrier, inc=1, device_id=where[side], device_id_type=MESH)

    look = lax.broadcasted_iota(jnp.int32, (128, columns), 1)
    cell = lax.broadcasted_iota(jnp.int32, (128, columns), 0)
    for tile in range(cells // 128):
        ones = jnp.where((cell + tile * 128) // LOOK_RG == look, 1.0, 0.0).astype(jnp.bfloat16)
        sel[tile, pl.ds(0, 128)] = ones
        sel[tile, pl.ds(128, 128)] = ones

    pl.semaphore_wait(barrier, count(greets[side] & jnp.logical_not(later[side]) for side in has))
    for side in has:
        @pl.when(greets[side] & (later[side] | former[side]))
        def _(side=side):
            pl.semaphore_signal(barrier, inc=1, device_id=where[side], device_id_type=MESH)

    def send(unit):
        for side in ("next", "prev"):
            @pl.when(has[side])
            def _(side=side):
                image_copy(side, unit).start()

    for unit in range(IN_FLIGHT):
        send(unit)

    for side, n in (("prev", 0), ("next", 1)):
        @pl.when(jnp.logical_not(has[side]))
        def _(n=n, side=side):
            far[n] = jnp.zeros(far.shape[1:], far.dtype)
            base = 3 if side == "prev" else 27
            results[base] = jnp.zeros(results.shape[1:], results.dtype)
            results[pl.ds(base + 3, 2)] = jnp.zeros((2,) + results.shape[1:], results.dtype)
    for side, n in (("low", 0), ("high", 1)):
        @pl.when(jnp.logical_not(has[side]))
        def _(n=n):
            halo[n] = jnp.zeros(halo.shape[1:], halo.dtype)

    def widen(source, target, row):
        def body(k, carry):
            lane = pl.ds(pl.multiple_of(k * 128, 128), 128)
            target[:, :, k] = source[:, :, row, lane].astype(jnp.float32)
            return carry

        lax.fori_loop(0, cells // 128, body, 0, unroll=2)

    def add_up(base, far_base, height, edges, dates, first, count):
        pairs = height // 2
        groups = edges if dates is None else [(edges, dates)]
        every = [e for pairs_of, _ in groups for e in pairs_of]
        needed = sorted({a for a, m in every} | {a + m for a, m in every})

        def body(k, total):
            packed = []
            weights = []
            for part in range(LANES // 128):
                tile = k * (LANES // 128) + part
                value = {}
                for a in needed:
                    value[a] = []
                    for c in range(2):
                        for odd in range(2):
                            row = pl.ds((base if 4 <= a < 8 else far_base) + odd, pairs, stride=2)
                            if 4 <= a < 8:
                                value[a].append(own_wide[c, a - 4, tile, row])
                            elif a < 4:
                                value[a].append(far_wide[0, c, a - 2, tile, row])
                            else:
                                value[a].append(far_wide[1, c, a - 8, tile, row])
                terms = []
                for pairs_of, alone in groups:
                    for a, m in pairs_of:
                        (x, z, y, w), (u, p, v, q) = value[a], value[a + m]
                        terms.append((x * u + y * v) + (z * p + w * q))
                        terms.append((y * u - x * v) + (w * p - z * q))
                    for a in alone:
                        x, z, y, w = value[a]
                        terms.append((x * x + y * y) + (z * z + w * w))
                left = jnp.concatenate(terms, axis=0)
                high = left.astype(jnp.bfloat16)
                low = (left - high.astype(jnp.float32)).astype(jnp.bfloat16)
                packed += [high, low]
                weights.append(sel[tile])
            left = jnp.concatenate(packed, axis=1)
            right = jnp.concatenate(weights, axis=0)
            return total + jnp.dot(left, right, preferred_element_type=jnp.float32)

        total = lax.fori_loop(0, cells // LANES, body, jnp.zeros((count * pairs, columns), jnp.float32))
        sums[pl.ds(first, count), pl.ds(PAD + base // 2, pairs), :] = total.reshape(count, pairs, columns)

    def windows(q, block):
        base = PAD + block * BLOCK * 2

        def every(shift):
            return sums[q, pl.ds(base + shift, BLOCK, stride=2), :]

        inner = every(0) + every(1)
        return inner, inner + (every(-1) + every(2))

    def finish(block, edges, power):
        for a, m in edges:
            for b in (a, a + m):
                if b not in power:
                    power[b] = windows(POWER[b], block)[1]
            look_re, win_re = windows(PLACE[a, m], block)
            look_im, win_im = windows(PLACE[a, m] + 1, block)
            size = jnp.sqrt(win_re * win_re + win_im * win_im)
            part = pl.ds(block * BLOCK, BLOCK)
            results[slot(a, m), 0, part] = look_re * (1.0 / (LOOK_AZ * LOOK_RG))
            results[slot(a, m), 1, part] = look_im * (1.0 / (LOOK_AZ * LOOK_RG))
            results[slot(a, m), 2, part] = size / jnp.sqrt(power[a] * power[a + m] + EPS)

    for step in range(rows // INNER_ROWS):
        own_copy(step).wait()
        row = pl.ds(step * INNER_ROWS, INNER_ROWS)
        widen(own, own_wide.at[:, :, :, row], row)
        add_up(step * INNER_ROWS, 0, INNER_ROWS, INNER, [4, 5, 6, 7], *SPAN["inner"])

    @pl.when(greets["high"] & later["high"])
    def _():
        pl.semaphore_wait(barrier, 1)

    def on_strip(which, body):
        for side, n in (("high", 0), ("low", 1)):
            @pl.when(has[side] & remote[side] & which)
            def _(side=side, n=n):
                body(side, n)

    def send_edges():
        for q in range(N_ALL):
            edge_sums[0, pl.ds(q, 1)] = sums[q, pl.ds(PAD + rows // 2 - 1, 1)]
            edge_sums[1, pl.ds(q, 1)] = sums[q, pl.ds(PAD, 1)]
        for side, n in (("high", 0), ("low", 1)):
            @pl.when(has[side] & jnp.logical_not(remote[side]))
            def _(side=side, n=n):
                halo_copy(n, edge_sums.at[n], side, halo_send.at[n]).start()
        on_strip(inner, lambda side, n: halo_copy(n, edge_sums.at[n], side, halo_send.at[n]).start())
        for at, toward in ((0, "next"), (3, "prev")):
            on_strip(place == at, lambda side, n, toward=toward: relay_out(n, toward).start())

    def relay_out(n, toward):
        return halo_copy(n, edge_sums.at[n], toward, relay_send.at[0], relayed.at[0], relay_recv.at[0])

    def relay_over(side, n):
        return halo_copy(n, relayed.at[0], side, relay_send.at[1], relayed.at[1], relay_recv.at[1])

    def relay_back(n, toward):
        return halo_copy(1 - n, relayed.at[1], toward, relay_send.at[2])

    def pass_over(side, n):
        relay_out(n, "next").wait_recv()
        relay_over(side, n).start()

    def pass_back():
        for at, toward in ((1, "prev"), (2, "next")):
            def body(side, n, toward=toward):
                relay_over(side, n).wait_recv()
                relay_back(n, toward).start()
            on_strip(place == at, body)

    def take_halo():
        for side, opposite, n in (("low", "high", 0), ("high", "low", 1)):
            @pl.when(has[side])
            def _(opposite=opposite, n=n):
                halo_copy(n, edge_sums.at[n], opposite, halo_send.at[n]).wait_recv()
        for q in range(N_ALL):
            sums[q, pl.ds(PAD - 1, 1)] = halo[0, pl.ds(q, 1)]
            sums[q, pl.ds(PAD + rows // 2, 1)] = halo[1, pl.ds(q, 1)]

    def finish_block(name, block):
        edges = INNER if name == "inner" else CROSS[name]
        power = {}
        for side in ("next", "prev"):
            owed = [e for e in edges if e in SHIPPED[side]]
            finish(block, owed, power)
            if owed:
                @pl.when(has[side])
                def _(side=side, owed=owed):
                    for edge in owed:
                        ship_copy(side, edge, block).start()
        finish(block, [e for e in edges if e not in SHIPPED["next"] + SHIPPED["prev"]], power)

    ready = {"inner": set(range(rows)), NEAR: set(), OTHER: set()}
    finished = set()
    for unit, (first, height, dates) in enumerate(UNITS):
        for side in ("prev", "next"):
            @pl.when(has[side])
            def _(side=side):
                image_copy("next" if side == "prev" else "prev", unit).wait_recv()
        if unit + IN_FLIGHT < len(UNITS):
            send(unit + IN_FLIGHT)
        if unit == HALO_AT:
            take_halo()
        row = pl.ds(first, height)
        for side, (low, high) in ((0, (2 - dates[1], 2 - dates[0])), (1, dates)):
            date = pl.ds(low, high - low)
            widen(far.at[side, :, date], far_wide.at[side, :, date, :, pl.ds(0, height)], row)
        names = [name for name in (NEAR, OTHER) if dates[0] <= name[0] and name[1] <= dates[1]]
        begin = SPAN[names[0]][0]
        number = sum(SPAN[name][1] for name in names)
        edges = [(CROSS[name], FAR[name]) for name in names]
        add_up(first, 0, height, edges, None, begin, number)
        for name in names:
            ready[name] |= set(range(first, first + height))
        if unit == EDGES_AT:
            send_edges()
        if unit == RELAY_AT[0]:
            on_strip(inner, pass_over)
        if unit == RELAY_AT[1]:
            pass_back()
        if unit > EDGES_AT:
            for name in (NEAR, OTHER, "inner"):
                for block in range(blocks):
                    height_of = BLOCK * LOOK_AZ
                    reach = set(range(max(block * height_of - 2, 0), min((block + 1) * height_of + 2, rows)))
                    inside = 0 < block < blocks - 1
                    late = (0 if name == "inner" else SHIP_AT) if inside else HALO_AT
                    if (name, block) not in finished and reach <= ready[name] and unit >= late:
                        finish_block(name, block)
                        finished.add((name, block))

    for side, opposite in (("next", "prev"), ("prev", "next")):
        @pl.when(has[side])
        def _(side=side, opposite=opposite):
            for block in range(blocks):
                for edge in SHIPPED[opposite]:
                    ship_copy(opposite, edge, block).wait_recv()

    offset_copy.wait()
    for i in range(OWN):
        for k in range(4):
            offset = offsets[i, k]
            place = 4 * (OWN + i + jnp.minimum(offset, 0)) + jnp.abs(offset) - 1
            sign = jnp.where(offset > 0, 1.0, -1.0)
            chosen = results[place]
            interferogram[i, k, 0] = chosen[0]
            interferogram[i, k, 1] = chosen[1] * sign
            coherence[i, k] = chosen[2]

    for side in ("next", "prev"):
        @pl.when(has[side])
        def _(side=side):
            for unit in range(len(UNITS)):
                image_copy(side, unit).wait_send()
            for block in range(blocks):
                for edge in SHIPPED[side]:
                    ship_copy(side, edge, block).wait_send()
    for side, n in (("high", 0), ("low", 1)):
        @pl.when(has[side] & (inner | jnp.logical_not(remote[side])))
        def _(side=side, n=n):
            halo_copy(n, edge_sums.at[n], side, halo_send.at[n]).wait_send()
    on_strip(jnp.logical_not(inner), lambda side, n: relay_out(n, "next").wait_send())
    on_strip(inner, lambda side, n: relay_over(side, n).wait_send())
    on_strip(inner, lambda side, n: relay_back(n, "next").wait_send())


def per_device(slc, partner_offset):
    _, dates, rows, cells = slc.shape
    columns = cells // LOOK_RG
    looks = rows // LOOK_AZ
    steps = rows // INNER_ROWS
    blocks = looks // BLOCK
    f32 = jnp.float32
    return pl.pallas_call(
        kernel,
        out_shape=(
            jax.ShapeDtypeStruct((dates, 4, 2, looks, columns), f32),
            jax.ShapeDtypeStruct((dates, 4, looks, columns), f32),
        ),
        in_specs=[
            pl.BlockSpec(memory_space=pltpu.HBM),
            pl.BlockSpec(memory_space=pltpu.HBM),
        ],
        out_specs=[pl.BlockSpec(memory_space=pltpu.VMEM)] * 2,
        scratch_shapes=[
            pltpu.SMEM(partner_offset.shape, partner_offset.dtype),
            pltpu.VMEM((2, dates, rows, cells), slc.dtype),
            pltpu.VMEM((2, 2, 2, rows, cells), slc.dtype),
            pltpu.VMEM((2, dates, cells // 128, rows, 128), f32),
            pltpu.VMEM((2, 2, 2, cells // 128, INNER_ROWS, 128), f32),
            pltpu.VMEM((cells // 128, 256, columns), jnp.bfloat16),
            pltpu.VMEM((N_ALL, rows // 2 + 2 * PAD, columns), f32),
            pltpu.VMEM((2, N_ALL, columns), f32),
            pltpu.VMEM((2, N_ALL, columns), f32),
            pltpu.VMEM((2, N_ALL, columns), f32),
            pltpu.VMEM((32, 3, looks, columns), f32),
            pltpu.SemaphoreType.DMA,
            pltpu.SemaphoreType.DMA((steps,)),
            pltpu.SemaphoreType.DMA((2, len(UNITS))),
            pltpu.SemaphoreType.DMA((2, len(UNITS))),
            pltpu.SemaphoreType.DMA((2,)),
            pltpu.SemaphoreType.DMA((2,)),
            pltpu.SemaphoreType.DMA((3,)),
            pltpu.SemaphoreType.DMA((2,)),
            pltpu.SemaphoreType.DMA((2, 3, blocks)),
            pltpu.SemaphoreType.DMA((2, 3, blocks)),
        ],
        compiler_params=pltpu.CompilerParams(
            collective_id=0, has_side_effects=True, vmem_limit_bytes=211 * 1024 * 256
        ),
    )(partner_offset, slc)


def solution(mesh):
    return jax.shard_map(
        per_device,
        mesh=mesh,
        in_specs=(P(None, "date", "strip", None), P("date", None)),
        out_specs=(P("date", None, None, "strip", None), P("date", None, "strip", None)),
        check_vma=False,
    )
```

```python
import functools

import jax
import jax.numpy as jnp
from jax import lax
from jax.experimental import pallas as pl
from jax.experimental.pallas import tpu as pltpu
from jax.sharding import PartitionSpec as P

MESH = pl.DeviceIdType.MESH
OWN = 4
MAXOFF = 4
LOOK_AZ = 4
LOOK_RG = 16
EPS = 1e-06
LANES = 1024
INNER_ROWS = 32
PAD = 8
BLOCK = 8
IN_FLIGHT = 3
BOTH, NEAR, OTHER = (0, 2), (0, 1), (1, 2)
UNITS = [(0, 16, BOTH), (112, 16, BOTH)]
UNITS += [(16, 32, NEAR), (48, 32, NEAR), (80, 32, NEAR)]
UNITS += [(80, 16, OTHER), (96, 16, OTHER), (48, 32, OTHER), (32, 16, OTHER), (16, 16, OTHER)]
LAST = len(UNITS) - 1
EDGES_AT = 1
RELAY_AT = (2, 4)
SHIFT = 5
BORROW_AT = 7
SHIP_AT = 7
HALO_AT = 8

INNER = [(a, m) for a in range(4, 8) for m in range(1, 5) if a + m < 8]
GROUPS = {
    "inner": [(INNER, [4, 5, 6, 7])],
    NEAR: [([(3, m) for m in range(1, 5)] + [(a, 8 - a) for a in range(4, 8)], [3, 8])],
    OTHER: [([(2, 4), (5, 4)], [2, 9]), ([(2, 2), (2, 3), (6, 3), (7, 2)], [])],
}
SHIPPED = {"next": [(4, 4), (5, 3), (5, 4)], "prev": [(3, 3), (3, 4), (2, 4)]}
TAIL = {"next": (5, 4), "prev": (2, 4)}
TAIL_BLOCKS = 2


def slot(a, m):
    return 4 * a + m - 1


PLACE = {}
POWER = {}
N_ALL = 0
for _groups in GROUPS.values():
    for _edges, _dates in _groups:
        for _edge in _edges:
            PLACE[_edge] = N_ALL
            N_ALL += 2
        for _date in _dates:
            POWER[_date] = N_ALL
            N_ALL += 1


def edges_of(name):
    return [edge for edges, _ in GROUPS[name] for edge in edges]


def kernel(
    partner_offset, slc, interferogram, coherence,
    offsets, own, far, own_wide, far_wide, sel, sums, edge_sums, halo, relayed, results, tail,
    extra, extra_wide, lent, borrowed,
    offset_sem, own_sem, send_sem, recv_sem, halo_send, halo_recv, relay_send, relay_recv, ship_send, ship_recv,
    tail_send, tail_recv, extra_sem, lend_sem,
):
    rows = own.shape[2]
    cells = own.shape[3]
    looks = rows // LOOK_AZ
    blocks = looks // BLOCK
    columns = cells // LOOK_RG
    d = lax.axis_index("date")
    s = lax.axis_index("strip")
    has = {
        "prev": d > 0,
        "next": d < lax.axis_size("date") - 1,
        "low": s > 0,
        "high": s < lax.axis_size("strip") - 1,
    }
    where = {
        "prev": {"date": d - 1},
        "next": {"date": d + 1},
        "low": {"strip": s - 1},
        "high": {"strip": s + 1},
    }
    place = d % 4
    inner = (place == 1) | (place == 2)
    remote = {"high": s % 2 == 1, "low": s % 2 == 0}
    greets = {
        "prev": has["prev"],
        "next": has["next"],
        "low": has["low"] & (inner | jnp.logical_not(remote["low"])),
        "high": has["high"] & (inner | jnp.logical_not(remote["high"])),
    }
    false = d < 0
    later = {"prev": false, "next": false, "low": false, "high": remote["high"]}
    former = {"prev": false, "next": false, "low": remote["low"], "high": false}

    turn = lax.axis_size("date") // 4
    early = (d % turn == 0) & (d > 0)
    late = (d % turn == turn - 1) & has["next"]

    def own_copy(step):
        part = (slice(None), slice(None), pl.ds(step * INNER_ROWS, INNER_ROWS))
        return pltpu.make_async_copy(slc.at[part], own.at[part], own_sem.at[step])

    def image_copy(side, unit):
        first, height, (low, high) = UNITS[unit]
        n = 0 if side == "next" else 1
        row = pl.ds(first, height)
        date = pl.ds(4 - high, high - low) if side == "next" else pl.ds(low, high - low)
        slots = pl.ds(2 - high, high - low) if side == "next" else pl.ds(low, high - low)
        return pltpu.make_async_remote_copy(
            src_ref=slc.at[:, date, row],
            dst_ref=far.at[n, :, slots, row],
            send_sem=send_sem.at[n, unit],
            recv_sem=recv_sem.at[n, unit],
            device_id=where[side],
            device_id_type=MESH,
        )

    def halo_copy(n, source, side, send, target=None, recv=None):
        return pltpu.make_async_remote_copy(
            src_ref=source,
            dst_ref=halo.at[n] if target is None else target,
            send_sem=send,
            recv_sem=halo_recv.at[n] if recv is None else recv,
            device_id=where[side],
            device_id_type=MESH,
        )

    def extra_copy():
        return pltpu.make_async_remote_copy(
            src_ref=slc.at[:, pl.ds(1, 1), pl.ds(UNITS[SHIFT][0], UNITS[SHIFT][1])],
            dst_ref=extra,
            send_sem=extra_sem.at[0],
            recv_sem=extra_sem.at[1],
            device_id=where["next"],
            device_id_type=MESH,
        )

    def lend_copy():
        return pltpu.make_async_remote_copy(
            src_ref=lent,
            dst_ref=borrowed,
            send_sem=lend_sem.at[0],
            recv_sem=lend_sem.at[1],
            device_id=where["prev"],
            device_id_type=MESH,
        )

    def tail_copy(side):
        n = 0 if side == "next" else 1
        return pltpu.make_async_remote_copy(
            src_ref=results.at[slot(*TAIL[side]), :, pl.ds(0, TAIL_BLOCKS * BLOCK)],
            dst_ref=tail.at[n],
            send_sem=tail_send.at[n],
            recv_sem=tail_recv.at[n],
            device_id=where[side],
            device_id_type=MESH,
        )

    def goes(side, unit):
        return has[side] & jnp.logical_not(early) if (side, unit) == ("prev", SHIFT) else has[side]

    def comes(side, unit):
        return has[side] & jnp.logical_not(late) if (side, unit) == ("next", SHIFT) else has[side]

    def ships(side, edge, block):
        return edge in SHIPPED[side] and not (edge == TAIL[side] and block < TAIL_BLOCKS)

    def ship_copy(side, edge, block):
        a, m = edge
        n, shift = (0, -16) if side == "next" else (1, 16)
        i = SHIPPED[side].index(edge)
        part = pl.ds(block * BLOCK, BLOCK)
        return pltpu.make_async_remote_copy(
            src_ref=results.at[slot(a, m), :, part],
            dst_ref=results.at[slot(a, m) + shift, :, part],
            send_sem=ship_send.at[n, i, block],
            recv_sem=ship_recv.at[n, i, block],
            device_id=where[side],
            device_id_type=MESH,
        )

    barrier = pltpu.get_barrier_semaphore()

    def count(flags):
        return sum(flag.astype(jnp.int32) for flag in flags)

    for side in has:
        @pl.when(greets[side] & jnp.logical_not(later[side] | former[side]))
        def _(side=side):
            pl.semaphore_signal(barrier, inc=1, device_id=where[side], device_id_type=MESH)

    offset_copy = pltpu.make_async_copy(partner_offset, offsets, offset_sem)
    for step in range(rows // INNER_ROWS):
        own_copy(step).start()
    offset_copy.start()

    look = lax.broadcasted_iota(jnp.int32, (128, columns), 1)
    cell = lax.broadcasted_iota(jnp.int32, (128, columns), 0)
    for tile in range(cells // 128):
        ones = jnp.where((cell + tile * 128) // LOOK_RG == look, 1.0, 0.0).astype(jnp.bfloat16)
        sel[tile, pl.ds(0, 128)] = ones
        sel[tile, pl.ds(128, 128)] = ones

    pl.semaphore_wait(barrier, count(greets[side] & jnp.logical_not(later[side]) for side in has))
    for side in has:
        @pl.when(greets[side] & (later[side] | former[side]))
        def _(side=side):
            pl.semaphore_signal(barrier, inc=1, device_id=where[side], device_id_type=MESH)

    def send(unit):
        for side in ("next", "prev"):
            @pl.when(goes(side, unit))
            def _(side=side):
                image_copy(side, unit).start()
        if unit == SHIFT:
            @pl.when(late)
            def _():
                extra_copy().start()

    for unit in range(IN_FLIGHT):
        send(unit)

    for side, n in (("prev", 0), ("next", 1)):
        @pl.when(jnp.logical_not(has[side]))
        def _(n=n, side=side):
            far[n] = jnp.zeros(far.shape[1:], far.dtype)
            base = 3 if side == "prev" else 27
            results[base] = jnp.zeros(results.shape[1:], results.dtype)
            results[pl.ds(base + 3, 2)] = jnp.zeros((2,) + results.shape[1:], results.dtype)
            tail[n] = jnp.zeros(tail.shape[1:], tail.dtype)
    for side in range(2):
        part = pl.ds(0, TAIL_BLOCKS * BLOCK)
        results[(7, 27)[side], :, part] = jnp.zeros(tail.shape[1:], results.dtype)
    @pl.when(late)
    def _():
        rows_of = pl.ds(UNITS[SHIFT][0], UNITS[SHIFT][1])
        far[1, :, 1, rows_of] = jnp.zeros((2, UNITS[SHIFT][1], cells), far.dtype)
    for side, n in (("low", 0), ("high", 1)):
        @pl.when(jnp.logical_not(has[side]))
        def _(n=n):
            halo[n] = jnp.zeros(halo.shape[1:], halo.dtype)

    def widen(source, target, row):
        def body(k, carry):
            lane = pl.ds(pl.multiple_of(k * 128, 128), 128)
            target[:, :, k] = source[:, :, row, lane].astype(jnp.float32)
            return carry

        lax.fori_loop(0, cells // 128, body, 0, unroll=2)

    def add_up(base, far_base, height, groups, output=None):
        pairs = height // 2
        first = PLACE.get(groups[0][0][0])
        count = sum(2 * len(edges) + len(dates) for edges, dates in groups)
        needed = sorted({b for edges, _ in groups for a, m in edges for b in (a, a + m)})

        def body(k, total):
            packed = []
            weights = []
            for part in range(LANES // 128):
                tile = k * (LANES // 128) + part
                value = {}
                for a in needed:
                    value[a] = []
                    for c in range(2):
                        for odd in range(2):
                            row = pl.ds((base if 4 <= a < 8 else far_base) + odd, pairs, stride=2)
                            if 4 <= a < 8:
                                value[a].append(own_wide[c, a - 4, tile, row])
                            elif a == 1:
                                value[a].append(extra_wide[c, 0, tile, row])
                            elif a < 4:
                                value[a].append(far_wide[0, c, a - 2, tile, row])
                            else:
                                value[a].append(far_wide[1, c, a - 8, tile, row])
                terms = []
                for pairs_of, alone in groups:
                    for a, m in pairs_of:
                        (x, z, y, w), (u, p, v, q) = value[a], value[a + m]
                        terms.append((x * u + y * v) + (z * p + w * q))
                        terms.append((y * u - x * v) + (w * p - z * q))
                    for a in alone:
                        x, z, y, w = value[a]
                        terms.append((x * x + y * y) + (z * z + w * w))
                left = jnp.concatenate(terms, axis=0)
                high = left.astype(jnp.bfloat16)
                low = (left - high.astype(jnp.float32)).astype(jnp.bfloat16)
                packed += [high, low]
                weights.append(sel[tile])
            left = jnp.concatenate(packed, axis=1)
            right = jnp.concatenate(weights, axis=0)
            return total + jnp.dot(left, right, preferred_element_type=jnp.float32)

        total = lax.fori_loop(0, cells // LANES, body, jnp.zeros((count * pairs, columns), jnp.float32))
        total = total.reshape(count, pairs, columns)
        if output is None:
            sums[pl.ds(first, count), pl.ds(PAD + base // 2, pairs), :] = total
        else:
            output[pl.ds(0, count)] = total

    def windows(q, block):
        base = PAD + block * BLOCK * 2

        def every(shift):
            return sums[q, pl.ds(base + shift, BLOCK, stride=2), :]

        inner = every(0) + every(1)
        return inner, inner + (every(-1) + every(2))

    def finish(block, edges, power):
        for a, m in edges:
            for b in (a, a + m):
                if b not in power:
                    power[b] = windows(POWER[b], block)[1]
            look_re, win_re = windows(PLACE[a, m], block)
            look_im, win_im = windows(PLACE[a, m] + 1, block)
            size = jnp.sqrt(win_re * win_re + win_im * win_im)
            part = pl.ds(block * BLOCK, BLOCK)
            results[slot(a, m), 0, part] = look_re * (1.0 / (LOOK_AZ * LOOK_RG))
            results[slot(a, m), 1, part] = look_im * (1.0 / (LOOK_AZ * LOOK_RG))
            results[slot(a, m), 2, part] = size / jnp.sqrt(power[a] * power[a + m] + EPS)

    for step in range(rows // INNER_ROWS):
        own_copy(step).wait()
        row = pl.ds(step * INNER_ROWS, INNER_ROWS)
        widen(own, own_wide.at[:, :, :, row], row)
        add_up(step * INNER_ROWS, 0, INNER_ROWS, GROUPS["inner"])

    @pl.when(greets["high"] & later["high"])
    def _():
        pl.semaphore_wait(barrier, 1)

    def on_strip(which, body):
        for side, n in (("high", 0), ("low", 1)):
            @pl.when(has[side] & remote[side] & which)
            def _(side=side, n=n):
                body(side, n)

    def send_edges():
        for q in range(N_ALL):
            edge_sums[0, pl.ds(q, 1)] = sums[q, pl.ds(PAD + rows // 2 - 1, 1)]
            edge_sums[1, pl.ds(q, 1)] = sums[q, pl.ds(PAD, 1)]
        for side, n in (("high", 0), ("low", 1)):
            @pl.when(has[side] & jnp.logical_not(remote[side]))
            def _(side=side, n=n):
                halo_copy(n, edge_sums.at[n], side, halo_send.at[n]).start()
        on_strip(inner, lambda side, n: halo_copy(n, edge_sums.at[n], side, halo_send.at[n]).start())
        for at, toward in ((0, "next"), (3, "prev")):
            on_strip(place == at, lambda side, n, toward=toward: relay_out(n, toward).start())

    def relay_out(n, toward):
        return halo_copy(n, edge_sums.at[n], toward, relay_send.at[0], relayed.at[0], relay_recv.at[0])

    def relay_over(side, n):
        return halo_copy(n, relayed.at[0], side, relay_send.at[1], relayed.at[1], relay_recv.at[1])

    def relay_back(n, toward):
        return halo_copy(1 - n, relayed.at[1], toward, relay_send.at[2])

    def pass_over(side, n):
        relay_out(n, "next").wait_recv()
        relay_over(side, n).start()

    def pass_back():
        for at, toward in ((1, "prev"), (2, "next")):
            def body(side, n, toward=toward):
                relay_over(side, n).wait_recv()
                relay_back(n, toward).start()
            on_strip(place == at, body)

    def take_halo():
        for side, opposite, n in (("low", "high", 0), ("high", "low", 1)):
            @pl.when(has[side])
            def _(opposite=opposite, n=n):
                halo_copy(n, edge_sums.at[n], opposite, halo_send.at[n]).wait_recv()
        for q in range(N_ALL):
            sums[q, pl.ds(PAD - 1, 1)] = halo[0, pl.ds(q, 1)]
            sums[q, pl.ds(PAD + rows // 2, 1)] = halo[1, pl.ds(q, 1)]

    def finish_block(name, block):
        power = {}
        edges = edges_of(name)
        for side in ("next", "prev"):
            owed = [edge for edge in edges if ships(side, edge, block)]
            finish(block, owed, power)
            if owed:
                @pl.when(has[side])
                def _(side=side, owed=owed):
                    for edge in owed:
                        ship_copy(side, edge, block).start()
        done = SHIPPED["next"] + SHIPPED["prev"]
        finish(block, [edge for edge in edges if edge not in done], power)

    def lend():
        first, height, _ = UNITS[SHIFT]
        extra_copy().wait_recv()
        widen(extra, extra_wide, pl.ds(0, height))
        add_up(first, 0, height, [([(1, 4)], [])], lent)
        row = pl.ds(PAD + first // 2, height // 2)
        for i, edge in enumerate(((2, 3), (3, 2))):
            lent[pl.ds(2 + 2 * i, 2)] = sums[pl.ds(PLACE[edge], 2), row]
        lent[6] = sums[POWER[5], row]
        lend_copy().start()

    def borrow():
        first, height, _ = UNITS[SHIFT]
        lend_copy().wait_recv()
        row = pl.ds(PAD + first // 2, height // 2)
        for i, edge in enumerate(((5, 4), (6, 3), (7, 2))):
            sums[pl.ds(PLACE[edge], 2), row] = borrowed[pl.ds(2 * i, 2)]
        sums[POWER[9], row] = borrowed[6]

    ready = {"inner": set(range(rows)), NEAR: set(), OTHER: set()}
    finished = set()
    for unit, (first, height, dates) in enumerate(UNITS):
        for side in ("prev", "next"):
            @pl.when(comes(side, unit))
            def _(side=side):
                image_copy("next" if side == "prev" else "prev", unit).wait_recv()
        if unit + IN_FLIGHT < len(UNITS):
            send(unit + IN_FLIGHT)
        if unit == HALO_AT:
            take_halo()
        if unit == BORROW_AT:
            pl.when(late)(borrow)
            ready[OTHER] |= set(range(UNITS[SHIFT][0], UNITS[SHIFT][0] + UNITS[SHIFT][1]))
        for side, (low, high) in ((0, (2 - dates[1], 2 - dates[0])), (1, dates)):
            date = pl.ds(low, high - low)
            widen(far.at[side, :, date], far_wide.at[side, :, date, :, pl.ds(0, height)], pl.ds(first, height))
        names = [name for name in (NEAR, OTHER) if dates[0] <= name[0] and name[1] <= dates[1]]
        if unit == LAST:
            add_up(first, 0, height, GROUPS[OTHER][:1])
            power = {}
            for side in ("next", "prev"):
                for block in range(TAIL_BLOCKS):
                    finish(block, [TAIL[side]], power.setdefault(block, {}))
                @pl.when(has[side])
                def _(side=side):
                    tail_copy(side).start()
            add_up(first, 0, height, GROUPS[OTHER][1:])
        else:
            add_up(first, 0, height, [group for name in names for group in GROUPS[name]])
        for name in names:
            if unit != SHIFT:
                ready[name] |= set(range(first, first + height))
        if unit == SHIFT:
            pl.when(early)(lend)
        if unit == EDGES_AT:
            send_edges()
        if unit == RELAY_AT[0]:
            on_strip(inner, pass_over)
        if unit == RELAY_AT[1]:
            pass_back()
        if unit > EDGES_AT:
            for name in (NEAR, OTHER, "inner"):
                for block in range(blocks):
                    height_of = BLOCK * LOOK_AZ
                    reach = set(range(max(block * height_of - 2, 0), min((block + 1) * height_of + 2, rows)))
                    inside = 0 < block < blocks - 1
                    least = (0 if name == "inner" else SHIP_AT) if inside else HALO_AT
                    if (name, block) not in finished and reach <= ready[name] and unit >= least:
                        finish_block(name, block)
                        finished.add((name, block))

    for side, opposite in (("next", "prev"), ("prev", "next")):
        @pl.when(has[side])
        def _(side=side, opposite=opposite):
            for block in range(blocks):
                for edge in SHIPPED[opposite]:
                    if ships(opposite, edge, block):
                        ship_copy(opposite, edge, block).wait_recv()

    offset_copy.wait()
    places = {}
    for i in range(OWN):
        for k in range(4):
            offset = offsets[i, k]
            place = 4 * (OWN + i + jnp.minimum(offset, 0)) + jnp.abs(offset) - 1
            sign = jnp.where(offset > 0, 1.0, -1.0)
            places[i, k] = place
            chosen = results[place]
            interferogram[i, k, 0] = chosen[0]
            interferogram[i, k, 1] = chosen[1] * sign
            coherence[i, k] = chosen[2]

    for n, side, i, sign in ((0, "prev", 1, -1.0), (1, "next", 2, 1.0)):
        @pl.when(has[side])
        def _(side=side):
            tail_copy("next" if side == "prev" else "prev").wait_recv()
        part = pl.ds(0, TAIL_BLOCKS * BLOCK)
        for k in range(4):
            here = places[i, k] == (7, 27)[n]
            interferogram[i, k, 0, part] = jnp.where(here, tail[n, 0], interferogram[i, k, 0, part])
            interferogram[i, k, 1, part] = jnp.where(here, tail[n, 1] * sign, interferogram[i, k, 1, part])
            coherence[i, k, part] = jnp.where(here, tail[n, 2], coherence[i, k, part])

    for side in ("next", "prev"):
        @pl.when(has[side])
        def _(side=side):
            for unit in range(len(UNITS)):
                if (side, unit) != ("prev", SHIFT):
                    image_copy(side, unit).wait_send()
            tail_copy(side).wait_send()
            for block in range(blocks):
                for edge in SHIPPED[side]:
                    if ships(side, edge, block):
                        ship_copy(side, edge, block).wait_send()
    @pl.when(goes("prev", SHIFT))
    def _():
        image_copy("prev", SHIFT).wait_send()
    @pl.when(late)
    def _():
        extra_copy().wait_send()
    @pl.when(early)
    def _():
        lend_copy().wait_send()
    for side, n in (("high", 0), ("low", 1)):
        @pl.when(has[side] & (inner | jnp.logical_not(remote[side])))
        def _(side=side, n=n):
            halo_copy(n, edge_sums.at[n], side, halo_send.at[n]).wait_send()
    on_strip(jnp.logical_not(inner), lambda side, n: relay_out(n, "next").wait_send())
    on_strip(inner, lambda side, n: relay_over(side, n).wait_send())
    on_strip(inner, lambda side, n: relay_back(n, "next").wait_send())


def per_device(slc, partner_offset):
    _, dates, rows, cells = slc.shape
    columns = cells // LOOK_RG
    looks = rows // LOOK_AZ
    steps = rows // INNER_ROWS
    blocks = looks // BLOCK
    f32 = jnp.float32
    return pl.pallas_call(
        kernel,
        out_shape=(
            jax.ShapeDtypeStruct((dates, 4, 2, looks, columns), f32),
            jax.ShapeDtypeStruct((dates, 4, looks, columns), f32),
        ),
        in_specs=[
            pl.BlockSpec(memory_space=pltpu.HBM),
            pl.BlockSpec(memory_space=pltpu.HBM),
        ],
        out_specs=[pl.BlockSpec(memory_space=pltpu.VMEM)] * 2,
        scratch_shapes=[
            pltpu.SMEM(partner_offset.shape, partner_offset.dtype),
            pltpu.VMEM((2, dates, rows, cells), slc.dtype),
            pltpu.VMEM((2, 2, 2, rows, cells), slc.dtype),
            pltpu.VMEM((2, dates, cells // 128, rows, 128), f32),
            pltpu.VMEM((2, 2, 2, cells // 128, INNER_ROWS, 128), f32),
            pltpu.VMEM((cells // 128, 256, columns), jnp.bfloat16),
            pltpu.VMEM((N_ALL, rows // 2 + 2 * PAD, columns), f32),
            pltpu.VMEM((2, N_ALL, columns), f32),
            pltpu.VMEM((2, N_ALL, columns), f32),
            pltpu.VMEM((2, N_ALL, columns), f32),
            pltpu.VMEM((32, 3, looks, columns), f32),
            pltpu.VMEM((2, 3, TAIL_BLOCKS * BLOCK, columns), f32),
            pltpu.VMEM((2, 1, UNITS[SHIFT][1], cells), slc.dtype),
            pltpu.VMEM((2, 1, cells // 128, UNITS[SHIFT][1], 128), f32),
            pltpu.VMEM((7, UNITS[SHIFT][1] // 2, columns), f32),
            pltpu.VMEM((7, UNITS[SHIFT][1] // 2, columns), f32),
            pltpu.SemaphoreType.DMA,
            pltpu.SemaphoreType.DMA((steps,)),
            pltpu.SemaphoreType.DMA((2, len(UNITS))),
            pltpu.SemaphoreType.DMA((2, len(UNITS))),
            pltpu.SemaphoreType.DMA((2,)),
            pltpu.SemaphoreType.DMA((2,)),
            pltpu.SemaphoreType.DMA((3,)),
            pltpu.SemaphoreType.DMA((2,)),
            pltpu.SemaphoreType.DMA((2, 3, blocks)),
            pltpu.SemaphoreType.DMA((2, 3, blocks)),
            pltpu.SemaphoreType.DMA((2,)),
            pltpu.SemaphoreType.DMA((2,)),
            pltpu.SemaphoreType.DMA((2,)),
            pltpu.SemaphoreType.DMA((2,)),
        ],
        compiler_params=pltpu.CompilerParams(
            collective_id=0, has_side_effects=True, vmem_limit_bytes=211 * 1024 * 256
        ),
    )(partner_offset, slc)


def solution(mesh):
    return jax.shard_map(
        per_device,
        mesh=mesh,
        in_specs=(P(None, "date", "strip", None), P("date", None)),
        out_specs=(P("date", None, None, "strip", None), P("date", None, "strip", None)),
        check_vma=False,
    )
```

```python
import functools

import jax
import jax.numpy as jnp
from jax import lax
from jax.experimental import pallas as pl
from jax.experimental.pallas import tpu as pltpu
from jax.sharding import PartitionSpec as P

MESH = pl.DeviceIdType.MESH
OWN = 4
MAXOFF = 4
LOOK_AZ = 4
LOOK_RG = 16
EPS = 1e-06
LANES = 1024
INNER_ROWS = 32
PAD = 8
BLOCK = 8
IN_FLIGHT = (3, 2)
CATCH_UP = 3
BOTH, NEAR, OTHER = (0, 2), (0, 1), (1, 2)
UNITS = [(0, 16, BOTH), (112, 16, BOTH)]
UNITS += [(16, 32, NEAR), (48, 32, NEAR), (80, 32, NEAR)]
UNITS += [(80, 16, OTHER), (96, 16, OTHER), (48, 32, OTHER), (32, 16, OTHER), (16, 16, OTHER)]
LAST = len(UNITS) - 1
EDGES_AT = 1
RELAY_AT = (2, 4)
SHIFT = 5
BORROW_AT = 7
SHIP_AT = 7
HALO_AT = 7

INNER = [(a, m) for a in range(4, 8) for m in range(1, 5) if a + m < 8]
GROUPS = {
    "inner": [(INNER, [4, 5, 6, 7])],
    NEAR: [([(3, m) for m in range(1, 5)] + [(a, 8 - a) for a in range(4, 8)], [3, 8])],
    OTHER: [([(2, 4), (5, 4)], [2, 9]), ([(2, 2), (2, 3), (6, 3), (7, 2)], [])],
}
SHIPPED = {"next": [(4, 4), (5, 3), (5, 4)], "prev": [(3, 3), (3, 4), (2, 4)]}
TAIL = {"next": (5, 4), "prev": (2, 4)}
TAIL_BLOCKS = 2


def slot(a, m):
    return 4 * a + m - 1


PLACE = {}
POWER = {}
N_ALL = 0
for _groups in GROUPS.values():
    for _edges, _dates in _groups:
        for _edge in _edges:
            PLACE[_edge] = N_ALL
            N_ALL += 2
        for _date in _dates:
            POWER[_date] = N_ALL
            N_ALL += 1


def edges_of(name):
    return [edge for edges, _ in GROUPS[name] for edge in edges]


def kernel(
    partner_offset, slc, interferogram, coherence,
    offsets, own, far, own_wide, far_wide, sel, sums, edge_sums, halo, relayed, results, tail,
    extra, extra_wide, lent, borrowed,
    offset_sem, own_sem, send_sem, recv_sem, halo_send, halo_recv, relay_send, relay_recv, ship_send, ship_recv,
    tail_send, tail_recv, extra_sem, lend_sem,
):
    rows = own.shape[2]
    cells = own.shape[3]
    looks = rows // LOOK_AZ
    blocks = looks // BLOCK
    columns = cells // LOOK_RG
    d = lax.axis_index("date")
    s = lax.axis_index("strip")
    has = {
        "prev": d > 0,
        "next": d < lax.axis_size("date") - 1,
        "low": s > 0,
        "high": s < lax.axis_size("strip") - 1,
    }
    where = {
        "prev": {"date": d - 1},
        "next": {"date": d + 1},
        "low": {"strip": s - 1},
        "high": {"strip": s + 1},
    }
    place = d % 4
    inner = (place == 1) | (place == 2)
    remote = {"high": s % 2 == 1, "low": s % 2 == 0}
    greets = {
        "prev": has["prev"],
        "next": has["next"],
        "low": has["low"] & (inner | jnp.logical_not(remote["low"])),
        "high": has["high"] & (inner | jnp.logical_not(remote["high"])),
    }
    false = d < 0
    later = {"prev": false, "next": false, "low": false, "high": remote["high"]}
    former = {"prev": false, "next": false, "low": remote["low"], "high": false}

    turn = lax.axis_size("date") // 4
    shifts = s < lax.axis_size("strip") // 2
    early = (d % turn == 0) & (d > 0) & shifts
    late = (d % turn == turn - 1) & has["next"] & shifts

    def own_copy(step):
        part = (slice(None), slice(None), pl.ds(step * INNER_ROWS, INNER_ROWS))
        return pltpu.make_async_copy(slc.at[part], own.at[part], own_sem.at[step])

    def image_copy(side, unit):
        first, height, (low, high) = UNITS[unit]
        n = 0 if side == "next" else 1
        row = pl.ds(first, height)
        date = pl.ds(4 - high, high - low) if side == "next" else pl.ds(low, high - low)
        slots = pl.ds(2 - high, high - low) if side == "next" else pl.ds(low, high - low)
        return pltpu.make_async_remote_copy(
            src_ref=slc.at[:, date, row],
            dst_ref=far.at[n, :, slots, row],
            send_sem=send_sem.at[n, unit],
            recv_sem=recv_sem.at[n, unit],
            device_id=where[side],
            device_id_type=MESH,
        )

    def halo_copy(n, source, side, send, target=None, recv=None):
        return pltpu.make_async_remote_copy(
            src_ref=source,
            dst_ref=halo.at[n] if target is None else target,
            send_sem=send,
            recv_sem=halo_recv.at[n] if recv is None else recv,
            device_id=where[side],
            device_id_type=MESH,
        )

    def extra_copy():
        return pltpu.make_async_remote_copy(
            src_ref=slc.at[:, pl.ds(1, 1), pl.ds(UNITS[SHIFT][0], UNITS[SHIFT][1])],
            dst_ref=extra,
            send_sem=extra_sem.at[0],
            recv_sem=extra_sem.at[1],
            device_id=where["next"],
            device_id_type=MESH,
        )

    def lend_copy():
        return pltpu.make_async_remote_copy(
            src_ref=lent,
            dst_ref=borrowed,
            send_sem=lend_sem.at[0],
            recv_sem=lend_sem.at[1],
            device_id=where["prev"],
            device_id_type=MESH,
        )

    def tail_copy(side):
        n = 0 if side == "next" else 1
        return pltpu.make_async_remote_copy(
            src_ref=results.at[slot(*TAIL[side]), :, pl.ds(0, TAIL_BLOCKS * BLOCK)],
            dst_ref=tail.at[n],
            send_sem=tail_send.at[n],
            recv_sem=tail_recv.at[n],
            device_id=where[side],
            device_id_type=MESH,
        )

    def goes(side, unit):
        return has[side] & jnp.logical_not(early) if (side, unit) == ("prev", SHIFT) else has[side]

    def comes(side, unit):
        return has[side] & jnp.logical_not(late) if (side, unit) == ("next", SHIFT) else has[side]

    def ships(side, edge, block):
        return edge in SHIPPED[side] and not (edge == TAIL[side] and block < TAIL_BLOCKS)

    def ship_copy(side, edge, block):
        a, m = edge
        n, shift = (0, -16) if side == "next" else (1, 16)
        i = SHIPPED[side].index(edge)
        part = pl.ds(block * BLOCK, BLOCK)
        return pltpu.make_async_remote_copy(
            src_ref=results.at[slot(a, m), :, part],
            dst_ref=results.at[slot(a, m) + shift, :, part],
            send_sem=ship_send.at[n, i, block],
            recv_sem=ship_recv.at[n, i, block],
            device_id=where[side],
            device_id_type=MESH,
        )

    barrier = pltpu.get_barrier_semaphore()

    def count(flags):
        return sum(flag.astype(jnp.int32) for flag in flags)

    for side in has:
        @pl.when(greets[side] & jnp.logical_not(later[side] | former[side]))
        def _(side=side):
            pl.semaphore_signal(barrier, inc=1, device_id=where[side], device_id_type=MESH)

    offset_copy = pltpu.make_async_copy(partner_offset, offsets, offset_sem)
    for step in range(rows // INNER_ROWS):
        own_copy(step).start()
    offset_copy.start()

    look = lax.broadcasted_iota(jnp.int32, (128, columns), 1)
    cell = lax.broadcasted_iota(jnp.int32, (128, columns), 0)
    for tile in range(cells // 128):
        ones = jnp.where((cell + tile * 128) // LOOK_RG == look, 1.0, 0.0).astype(jnp.bfloat16)
        sel[tile, pl.ds(0, 128)] = ones
        sel[tile, pl.ds(128, 128)] = ones

    pl.semaphore_wait(barrier, count(greets[side] & jnp.logical_not(later[side]) for side in has))
    for side in has:
        @pl.when(greets[side] & (later[side] | former[side]))
        def _(side=side):
            pl.semaphore_signal(barrier, inc=1, device_id=where[side], device_id_type=MESH)

    def send(unit, device):
        for side in ("next", "prev"):
            @pl.when(goes(side, unit) & (s % 2 == device))
            def _(side=side):
                image_copy(side, unit).start()
        if unit == SHIFT:
            @pl.when(late & (s % 2 == device))
            def _():
                extra_copy().start()

    for device in range(2):
        for unit in range(IN_FLIGHT[device]):
            send(unit, device)
    started = list(IN_FLIGHT)

    for side, n in (("prev", 0), ("next", 1)):
        @pl.when(jnp.logical_not(has[side]))
        def _(n=n, side=side):
            far[n] = jnp.zeros(far.shape[1:], far.dtype)
            base = 3 if side == "prev" else 27
            results[base] = jnp.zeros(results.shape[1:], results.dtype)
            results[pl.ds(base + 3, 2)] = jnp.zeros((2,) + results.shape[1:], results.dtype)
            tail[n] = jnp.zeros(tail.shape[1:], tail.dtype)
    for side in range(2):
        part = pl.ds(0, TAIL_BLOCKS * BLOCK)
        results[(7, 27)[side], :, part] = jnp.zeros(tail.shape[1:], results.dtype)
    @pl.when(late)
    def _():
        rows_of = pl.ds(UNITS[SHIFT][0], UNITS[SHIFT][1])
        far[1, :, 1, rows_of] = jnp.zeros((2, UNITS[SHIFT][1], cells), far.dtype)
    for side, n in (("low", 0), ("high", 1)):
        @pl.when(jnp.logical_not(has[side]))
        def _(n=n):
            halo[n] = jnp.zeros(halo.shape[1:], halo.dtype)

    def widen(source, target, row):
        def body(k, carry):
            lane = pl.ds(pl.multiple_of(k * 128, 128), 128)
            target[:, :, k] = source[:, :, row, lane].astype(jnp.float32)
            return carry

        lax.fori_loop(0, cells // 128, body, 0, unroll=2)

    def add_up(base, far_base, height, groups, output=None):
        pairs = height // 2
        first = PLACE.get(groups[0][0][0])
        count = sum(2 * len(edges) + len(dates) for edges, dates in groups)
        needed = sorted({b for edges, _ in groups for a, m in edges for b in (a, a + m)})

        def body(k, total):
            packed = []
            weights = []
            for part in range(LANES // 128):
                tile = k * (LANES // 128) + part
                value = {}
                for a in needed:
                    value[a] = []
                    for c in range(2):
                        for odd in range(2):
                            row = pl.ds((base if 4 <= a < 8 else far_base) + odd, pairs, stride=2)
                            if 4 <= a < 8:
                                value[a].append(own_wide[c, a - 4, tile, row])
                            elif a == 1:
                                value[a].append(extra_wide[c, 0, tile, row])
                            elif a < 4:
                                value[a].append(far_wide[0, c, a - 2, tile, row])
                            else:
                                value[a].append(far_wide[1, c, a - 8, tile, row])
                terms = []
                for pairs_of, alone in groups:
                    for a, m in pairs_of:
                        (x, z, y, w), (u, p, v, q) = value[a], value[a + m]
                        terms.append((x * u + y * v) + (z * p + w * q))
                        terms.append((y * u - x * v) + (w * p - z * q))
                    for a in alone:
                        x, z, y, w = value[a]
                        terms.append((x * x + y * y) + (z * z + w * w))
                left = jnp.concatenate(terms, axis=0)
                high = left.astype(jnp.bfloat16)
                low = (left - high.astype(jnp.float32)).astype(jnp.bfloat16)
                packed += [high, low]
                weights.append(sel[tile])
            left = jnp.concatenate(packed, axis=1)
            right = jnp.concatenate(weights, axis=0)
            return total + jnp.dot(left, right, preferred_element_type=jnp.float32)

        total = lax.fori_loop(0, cells // LANES, body, jnp.zeros((count * pairs, columns), jnp.float32))
        total = total.reshape(count, pairs, columns)
        if output is None:
            sums[pl.ds(first, count), pl.ds(PAD + base // 2, pairs), :] = total
        else:
            output[pl.ds(0, count)] = total

    def windows(q, block):
        base = PAD + block * BLOCK * 2

        def every(shift):
            return sums[q, pl.ds(base + shift, BLOCK, stride=2), :]

        inner = every(0) + every(1)
        return inner, inner + (every(-1) + every(2))

    def finish(block, edges, power):
        for a, m in edges:
            for b in (a, a + m):
                if b not in power:
                    power[b] = windows(POWER[b], block)[1]
            look_re, win_re = windows(PLACE[a, m], block)
            look_im, win_im = windows(PLACE[a, m] + 1, block)
            size = jnp.sqrt(win_re * win_re + win_im * win_im)
            part = pl.ds(block * BLOCK, BLOCK)
            results[slot(a, m), 0, part] = look_re * (1.0 / (LOOK_AZ * LOOK_RG))
            results[slot(a, m), 1, part] = look_im * (1.0 / (LOOK_AZ * LOOK_RG))
            results[slot(a, m), 2, part] = size / jnp.sqrt(power[a] * power[a + m] + EPS)

    for step in range(rows // INNER_ROWS):
        own_copy(step).wait()
        row = pl.ds(step * INNER_ROWS, INNER_ROWS)
        widen(own, own_wide.at[:, :, :, row], row)
        add_up(step * INNER_ROWS, 0, INNER_ROWS, GROUPS["inner"])

    @pl.when(greets["high"] & later["high"])
    def _():
        pl.semaphore_wait(barrier, 1)

    def on_strip(which, body):
        for side, n in (("high", 0), ("low", 1)):
            @pl.when(has[side] & remote[side] & which)
            def _(side=side, n=n):
                body(side, n)

    def send_edges():
        for q in range(N_ALL):
            edge_sums[0, pl.ds(q, 1)] = sums[q, pl.ds(PAD + rows // 2 - 1, 1)]
            edge_sums[1, pl.ds(q, 1)] = sums[q, pl.ds(PAD, 1)]
        for side, n in (("high", 0), ("low", 1)):
            @pl.when(has[side] & jnp.logical_not(remote[side]))
            def _(side=side, n=n):
                halo_copy(n, edge_sums.at[n], side, halo_send.at[n]).start()
        on_strip(inner, lambda side, n: halo_copy(n, edge_sums.at[n], side, halo_send.at[n]).start())
        for at, toward in ((0, "next"), (3, "prev")):
            on_strip(place == at, lambda side, n, toward=toward: relay_out(n, toward).start())

    def relay_out(n, toward):
        return halo_copy(n, edge_sums.at[n], toward, relay_send.at[0], relayed.at[0], relay_recv.at[0])

    def relay_over(side, n):
        return halo_copy(n, relayed.at[0], side, relay_send.at[1], relayed.at[1], relay_recv.at[1])

    def relay_back(n, toward):
        return halo_copy(1 - n, relayed.at[1], toward, relay_send.at[2])

    def pass_over(side, n):
        relay_out(n, "next").wait_recv()
        relay_over(side, n).start()

    def pass_back():
        for at, toward in ((1, "prev"), (2, "next")):
            def body(side, n, toward=toward):
                relay_over(side, n).wait_recv()
                relay_back(n, toward).start()
            on_strip(place == at, body)

    def take_halo():
        for side, opposite, n in (("low", "high", 0), ("high", "low", 1)):
            @pl.when(has[side])
            def _(opposite=opposite, n=n):
                halo_copy(n, edge_sums.at[n], opposite, halo_send.at[n]).wait_recv()
        for q in range(N_ALL):
            sums[q, pl.ds(PAD - 1, 1)] = halo[0, pl.ds(q, 1)]
            sums[q, pl.ds(PAD + rows // 2, 1)] = halo[1, pl.ds(q, 1)]

    def finish_block(name, block):
        power = {}
        edges = edges_of(name)
        for side in ("next", "prev"):
            owed = [edge for edge in edges if ships(side, edge, block)]
            finish(block, owed, power)
            if owed:
                @pl.when(has[side])
                def _(side=side, owed=owed):
                    for edge in owed:
                        ship_copy(side, edge, block).start()
        done = SHIPPED["next"] + SHIPPED["prev"]
        finish(block, [edge for edge in edges if edge not in done], power)

    def lend():
        first, height, _ = UNITS[SHIFT]
        extra_copy().wait_recv()
        widen(extra, extra_wide, pl.ds(0, height))
        add_up(first, 0, height, [([(1, 4)], [])], lent)
        row = pl.ds(PAD + first // 2, height // 2)
        for i, edge in enumerate(((2, 3), (3, 2))):
            lent[pl.ds(2 + 2 * i, 2)] = sums[pl.ds(PLACE[edge], 2), row]
        lent[6] = sums[POWER[5], row]
        lend_copy().start()

    def borrow():
        first, height, _ = UNITS[SHIFT]
        lend_copy().wait_recv()
        row = pl.ds(PAD + first // 2, height // 2)
        for i, edge in enumerate(((5, 4), (6, 3), (7, 2))):
            sums[pl.ds(PLACE[edge], 2), row] = borrowed[pl.ds(2 * i, 2)]
        sums[POWER[9], row] = borrowed[6]

    ready = {"inner": set(range(rows)), NEAR: set(), OTHER: set()}
    finished = set()
    for unit, (first, height, dates) in enumerate(UNITS):
        for side in ("prev", "next"):
            @pl.when(comes(side, unit))
            def _(side=side):
                image_copy("next" if side == "prev" else "prev", unit).wait_recv()
        for device in range(2):
            ahead = IN_FLIGHT[0 if unit >= CATCH_UP else device]
            while started[device] < min(unit + 1 + ahead, len(UNITS)):
                send(started[device], device)
                started[device] += 1
        if unit == HALO_AT:
            take_halo()
        if unit == BORROW_AT:
            pl.when(late)(borrow)
            ready[OTHER] |= set(range(UNITS[SHIFT][0], UNITS[SHIFT][0] + UNITS[SHIFT][1]))
        for side, (low, high) in ((0, (2 - dates[1], 2 - dates[0])), (1, dates)):
            date = pl.ds(low, high - low)
            widen(far.at[side, :, date], far_wide.at[side, :, date, :, pl.ds(0, height)], pl.ds(first, height))
        names = [name for name in (NEAR, OTHER) if dates[0] <= name[0] and name[1] <= dates[1]]
        if unit == LAST:
            add_up(first, 0, height, GROUPS[OTHER][:1])
            power = {}
            for side in ("next", "prev"):
                for block in range(TAIL_BLOCKS):
                    finish(block, [TAIL[side]], power.setdefault(block, {}))
                @pl.when(has[side])
                def _(side=side):
                    tail_copy(side).start()
            add_up(first, 0, height, GROUPS[OTHER][1:])
        else:
            add_up(first, 0, height, [group for name in names for group in GROUPS[name]])
        for name in names:
            if unit != SHIFT:
                ready[name] |= set(range(first, first + height))
        if unit == SHIFT:
            pl.when(early)(lend)
        if unit == EDGES_AT:
            send_edges()
        if unit == RELAY_AT[0]:
            on_strip(inner, pass_over)
        if unit == RELAY_AT[1]:
            pass_back()
        if unit > EDGES_AT:
            for name in (NEAR, OTHER, "inner"):
                for block in range(blocks):
                    height_of = BLOCK * LOOK_AZ
                    reach = set(range(max(block * height_of - 2, 0), min((block + 1) * height_of + 2, rows)))
                    inside = 0 < block < blocks - 1
                    least = (0 if inside else LAST) if name == "inner" else (SHIP_AT if inside else HALO_AT)
                    if (name, block) not in finished and reach <= ready[name] and unit >= least:
                        finish_block(name, block)
                        finished.add((name, block))

    for side, opposite in (("next", "prev"), ("prev", "next")):
        @pl.when(has[side])
        def _(side=side, opposite=opposite):
            for block in range(blocks):
                for edge in SHIPPED[opposite]:
                    if ships(opposite, edge, block):
                        ship_copy(opposite, edge, block).wait_recv()

    offset_copy.wait()
    places = {}
    for i in range(OWN):
        for k in range(4):
            offset = offsets[i, k]
            place = 4 * (OWN + i + jnp.minimum(offset, 0)) + jnp.abs(offset) - 1
            sign = jnp.where(offset > 0, 1.0, -1.0)
            places[i, k] = place
            chosen = results[place]
            interferogram[i, k, 0] = chosen[0]
            interferogram[i, k, 1] = chosen[1] * sign
            coherence[i, k] = chosen[2]

    for n, side, i, sign in ((0, "prev", 1, -1.0), (1, "next", 2, 1.0)):
        @pl.when(has[side])
        def _(side=side):
            tail_copy("next" if side == "prev" else "prev").wait_recv()
        part = pl.ds(0, TAIL_BLOCKS * BLOCK)
        for k in range(4):
            here = places[i, k] == (7, 27)[n]
            interferogram[i, k, 0, part] = jnp.where(here, tail[n, 0], interferogram[i, k, 0, part])
            interferogram[i, k, 1, part] = jnp.where(here, tail[n, 1] * sign, interferogram[i, k, 1, part])
            coherence[i, k, part] = jnp.where(here, tail[n, 2], coherence[i, k, part])

    for side in ("next", "prev"):
        @pl.when(has[side])
        def _(side=side):
            for unit in range(len(UNITS)):
                if (side, unit) != ("prev", SHIFT):
                    image_copy(side, unit).wait_send()
            tail_copy(side).wait_send()
            for block in range(blocks):
                for edge in SHIPPED[side]:
                    if ships(side, edge, block):
                        ship_copy(side, edge, block).wait_send()
    @pl.when(goes("prev", SHIFT))
    def _():
        image_copy("prev", SHIFT).wait_send()
    @pl.when(late)
    def _():
        extra_copy().wait_send()
    @pl.when(early)
    def _():
        lend_copy().wait_send()
    for side, n in (("high", 0), ("low", 1)):
        @pl.when(has[side] & (inner | jnp.logical_not(remote[side])))
        def _(side=side, n=n):
            halo_copy(n, edge_sums.at[n], side, halo_send.at[n]).wait_send()
    on_strip(jnp.logical_not(inner), lambda side, n: relay_out(n, "next").wait_send())
    on_strip(inner, lambda side, n: relay_over(side, n).wait_send())
    on_strip(inner, lambda side, n: relay_back(n, "next").wait_send())


def per_device(slc, partner_offset):
    _, dates, rows, cells = slc.shape
    columns = cells // LOOK_RG
    looks = rows // LOOK_AZ
    steps = rows // INNER_ROWS
    blocks = looks // BLOCK
    f32 = jnp.float32
    return pl.pallas_call(
        kernel,
        out_shape=(
            jax.ShapeDtypeStruct((dates, 4, 2, looks, columns), f32),
            jax.ShapeDtypeStruct((dates, 4, looks, columns), f32),
        ),
        in_specs=[
            pl.BlockSpec(memory_space=pltpu.HBM),
            pl.BlockSpec(memory_space=pltpu.HBM),
        ],
        out_specs=[pl.BlockSpec(memory_space=pltpu.VMEM)] * 2,
        scratch_shapes=[
            pltpu.SMEM(partner_offset.shape, partner_offset.dtype),
            pltpu.VMEM((2, dates, rows, cells), slc.dtype),
            pltpu.VMEM((2, 2, 2, rows, cells), slc.dtype),
            pltpu.VMEM((2, dates, cells // 128, rows, 128), f32),
            pltpu.VMEM((2, 2, 2, cells // 128, INNER_ROWS, 128), f32),
            pltpu.VMEM((cells // 128, 256, columns), jnp.bfloat16),
            pltpu.VMEM((N_ALL, rows // 2 + 2 * PAD, columns), f32),
            pltpu.VMEM((2, N_ALL, columns), f32),
            pltpu.VMEM((2, N_ALL, columns), f32),
            pltpu.VMEM((2, N_ALL, columns), f32),
            pltpu.VMEM((32, 3, looks, columns), f32),
            pltpu.VMEM((2, 3, TAIL_BLOCKS * BLOCK, columns), f32),
            pltpu.VMEM((2, 1, UNITS[SHIFT][1], cells), slc.dtype),
            pltpu.VMEM((2, 1, cells // 128, UNITS[SHIFT][1], 128), f32),
            pltpu.VMEM((7, UNITS[SHIFT][1] // 2, columns), f32),
            pltpu.VMEM((7, UNITS[SHIFT][1] // 2, columns), f32),
            pltpu.SemaphoreType.DMA,
            pltpu.SemaphoreType.DMA((steps,)),
            pltpu.SemaphoreType.DMA((2, len(UNITS))),
            pltpu.SemaphoreType.DMA((2, len(UNITS))),
            pltpu.SemaphoreType.DMA((2,)),
            pltpu.SemaphoreType.DMA((2,)),
            pltpu.SemaphoreType.DMA((3,)),
            pltpu.SemaphoreType.DMA((2,)),
            pltpu.SemaphoreType.DMA((2, 3, blocks)),
            pltpu.SemaphoreType.DMA((2, 3, blocks)),
            pltpu.SemaphoreType.DMA((2,)),
            pltpu.SemaphoreType.DMA((2,)),
            pltpu.SemaphoreType.DMA((2,)),
            pltpu.SemaphoreType.DMA((2,)),
        ],
        compiler_params=pltpu.CompilerParams(
            collective_id=0, has_side_effects=True, vmem_limit_bytes=211 * 1024 * 256
        ),
    )(partner_offset, slc)


def solution(mesh):
    return jax.shard_map(
        per_device,
        mesh=mesh,
        in_specs=(P(None, "date", "strip", None), P("date", None)),
        out_specs=(P("date", None, None, "strip", None), P("date", None, "strip", None)),
        check_vma=False,
    )
```

```python
import functools

import jax
import jax.numpy as jnp
from jax import lax
from jax.experimental import pallas as pl
from jax.experimental.pallas import tpu as pltpu
from jax.sharding import PartitionSpec as P

MESH = pl.DeviceIdType.MESH
OWN = 4
MAXOFF = 4
LOOK_AZ = 4
LOOK_RG = 16
EPS = 1e-06
LANES = 1024
INNER_ROWS = 32
PAD = 8
BLOCK = 8
IN_FLIGHT = (3, 2)
CATCH_UP = 3
BOTH, NEAR, OTHER = (0, 2), (0, 1), (1, 2)
UNITS = [(0, 16, BOTH), (112, 16, BOTH)]
UNITS += [(16, 32, NEAR), (48, 32, NEAR), (80, 32, NEAR)]
UNITS += [(80, 16, OTHER), (96, 16, OTHER), (48, 32, OTHER), (32, 16, OTHER), (16, 16, OTHER)]
LAST = len(UNITS) - 1
EDGES_AT = 1
RELAY_AT = (2, 4)
SHIFT = 5
BORROW_AT = 7
SHIP_AT = 7
HALO_AT = 7

INNER = [(a, m) for a in range(4, 8) for m in range(1, 5) if a + m < 8]
GROUPS = {
    "inner": [(INNER, [4, 5, 6, 7])],
    NEAR: [([(3, m) for m in range(1, 5)] + [(a, 8 - a) for a in range(4, 8)], [3, 8])],
    OTHER: [([(5, 4)], [9]), ([(2, 4)], [2]), ([(2, 2), (2, 3), (6, 3), (7, 2)], [])],
}
SHIPPED = {"next": [(4, 4), (5, 3), (5, 4)], "prev": [(3, 3), (3, 4), (2, 4)]}
TAIL = {"next": (5, 4), "prev": (2, 4)}
TAIL_BLOCKS = 2


def slot(a, m):
    return 4 * a + m - 1


PLACE = {}
POWER = {}
N_ALL = 0
for _groups in GROUPS.values():
    for _edges, _dates in _groups:
        for _edge in _edges:
            PLACE[_edge] = N_ALL
            N_ALL += 2
        for _date in _dates:
            POWER[_date] = N_ALL
            N_ALL += 1


def edges_of(name):
    return [edge for edges, _ in GROUPS[name] for edge in edges]


def kernel(
    partner_offset, slc, interferogram, coherence,
    offsets, own, far, own_wide, far_wide, sel, sums, edge_sums, halo, relayed, results, tail,
    extra, extra_wide, lent, borrowed,
    offset_sem, own_sem, send_sem, recv_sem, halo_send, halo_recv, relay_send, relay_recv, ship_send, ship_recv,
    tail_send, tail_recv, extra_sem, lend_sem,
):
    rows = own.shape[2]
    cells = own.shape[3]
    looks = rows // LOOK_AZ
    blocks = looks // BLOCK
    columns = cells // LOOK_RG
    d = lax.axis_index("date")
    s = lax.axis_index("strip")
    has = {
        "prev": d > 0,
        "next": d < lax.axis_size("date") - 1,
        "low": s > 0,
        "high": s < lax.axis_size("strip") - 1,
    }
    where = {
        "prev": {"date": d - 1},
        "next": {"date": d + 1},
        "low": {"strip": s - 1},
        "high": {"strip": s + 1},
    }
    place = d % 4
    inner = (place == 1) | (place == 2)
    remote = {"high": s % 2 == 1, "low": s % 2 == 0}
    greets = {
        "prev": has["prev"],
        "next": has["next"],
        "low": has["low"] & (inner | jnp.logical_not(remote["low"])),
        "high": has["high"] & (inner | jnp.logical_not(remote["high"])),
    }
    false = d < 0
    later = {"prev": false, "next": false, "low": false, "high": remote["high"]}
    former = {"prev": false, "next": false, "low": remote["low"], "high": false}

    turn = lax.axis_size("date") // 4
    shifts = s < lax.axis_size("strip") // 2
    early = (d % turn == 0) & (d > 0) & shifts
    late = (d % turn == turn - 1) & has["next"] & shifts

    def own_copy(step):
        part = (slice(None), slice(None), pl.ds(step * INNER_ROWS, INNER_ROWS))
        return pltpu.make_async_copy(slc.at[part], own.at[part], own_sem.at[step])

    def image_copy(side, unit):
        first, height, (low, high) = UNITS[unit]
        n = 0 if side == "next" else 1
        row = pl.ds(first, height)
        date = pl.ds(4 - high, high - low) if side == "next" else pl.ds(low, high - low)
        slots = pl.ds(2 - high, high - low) if side == "next" else pl.ds(low, high - low)
        return pltpu.make_async_remote_copy(
            src_ref=slc.at[:, date, row],
            dst_ref=far.at[n, :, slots, row],
            send_sem=send_sem.at[n, unit],
            recv_sem=recv_sem.at[n, unit],
            device_id=where[side],
            device_id_type=MESH,
        )

    def halo_copy(n, source, side, send, target=None, recv=None):
        return pltpu.make_async_remote_copy(
            src_ref=source,
            dst_ref=halo.at[n] if target is None else target,
            send_sem=send,
            recv_sem=halo_recv.at[n] if recv is None else recv,
            device_id=where[side],
            device_id_type=MESH,
        )

    def extra_copy():
        return pltpu.make_async_remote_copy(
            src_ref=slc.at[:, pl.ds(1, 1), pl.ds(UNITS[SHIFT][0], UNITS[SHIFT][1])],
            dst_ref=extra,
            send_sem=extra_sem.at[0],
            recv_sem=extra_sem.at[1],
            device_id=where["next"],
            device_id_type=MESH,
        )

    def lend_copy():
        return pltpu.make_async_remote_copy(
            src_ref=lent,
            dst_ref=borrowed,
            send_sem=lend_sem.at[0],
            recv_sem=lend_sem.at[1],
            device_id=where["prev"],
            device_id_type=MESH,
        )

    def tail_copy(side):
        n = 0 if side == "next" else 1
        return pltpu.make_async_remote_copy(
            src_ref=results.at[slot(*TAIL[side]), :, pl.ds(0, TAIL_BLOCKS * BLOCK)],
            dst_ref=tail.at[n],
            send_sem=tail_send.at[n],
            recv_sem=tail_recv.at[n],
            device_id=where[side],
            device_id_type=MESH,
        )

    def goes(side, unit):
        return has[side] & jnp.logical_not(early) if (side, unit) == ("prev", SHIFT) else has[side]

    def comes(side, unit):
        return has[side] & jnp.logical_not(late) if (side, unit) == ("next", SHIFT) else has[side]

    def ships(side, edge, block):
        return edge in SHIPPED[side] and not (edge == TAIL[side] and block < TAIL_BLOCKS)

    def ship_copy(side, edge, block):
        a, m = edge
        n, shift = (0, -16) if side == "next" else (1, 16)
        i = SHIPPED[side].index(edge)
        part = pl.ds(block * BLOCK, BLOCK)
        return pltpu.make_async_remote_copy(
            src_ref=results.at[slot(a, m), :, part],
            dst_ref=results.at[slot(a, m) + shift, :, part],
            send_sem=ship_send.at[n, i, block],
            recv_sem=ship_recv.at[n, i, block],
            device_id=where[side],
            device_id_type=MESH,
        )

    barrier = pltpu.get_barrier_semaphore()

    def count(flags):
        return sum(flag.astype(jnp.int32) for flag in flags)

    for side in has:
        @pl.when(greets[side] & jnp.logical_not(later[side] | former[side]))
        def _(side=side):
            pl.semaphore_signal(barrier, inc=1, device_id=where[side], device_id_type=MESH)

    offset_copy = pltpu.make_async_copy(partner_offset, offsets, offset_sem)
    for step in range(rows // INNER_ROWS):
        own_copy(step).start()
    offset_copy.start()

    look = lax.broadcasted_iota(jnp.int32, (128, columns), 1)
    cell = lax.broadcasted_iota(jnp.int32, (128, columns), 0)
    for tile in range(cells // 128):
        ones = jnp.where((cell + tile * 128) // LOOK_RG == look, 1.0, 0.0).astype(jnp.bfloat16)
        sel[tile, pl.ds(0, 128)] = ones
        sel[tile, pl.ds(128, 128)] = ones

    pl.semaphore_wait(barrier, count(greets[side] & jnp.logical_not(later[side]) for side in has))
    for side in has:
        @pl.when(greets[side] & (later[side] | former[side]))
        def _(side=side):
            pl.semaphore_signal(barrier, inc=1, device_id=where[side], device_id_type=MESH)

    def send(unit, device):
        for side in ("next", "prev"):
            @pl.when(goes(side, unit) & (s % 2 == device))
            def _(side=side):
                image_copy(side, unit).start()
        if unit == SHIFT:
            @pl.when(late & (s % 2 == device))
            def _():
                extra_copy().start()

    for device in range(2):
        for unit in range(IN_FLIGHT[device]):
            send(unit, device)
    started = list(IN_FLIGHT)

    for side, n in (("prev", 0), ("next", 1)):
        @pl.when(jnp.logical_not(has[side]))
        def _(n=n, side=side):
            far[n] = jnp.zeros(far.shape[1:], far.dtype)
            base = 3 if side == "prev" else 27
            results[base] = jnp.zeros(results.shape[1:], results.dtype)
            results[pl.ds(base + 3, 2)] = jnp.zeros((2,) + results.shape[1:], results.dtype)
            tail[n] = jnp.zeros(tail.shape[1:], tail.dtype)
    for side in range(2):
        part = pl.ds(0, TAIL_BLOCKS * BLOCK)
        results[(7, 27)[side], :, part] = jnp.zeros(tail.shape[1:], results.dtype)
    @pl.when(late)
    def _():
        rows_of = pl.ds(UNITS[SHIFT][0], UNITS[SHIFT][1])
        far[1, :, 1, rows_of] = jnp.zeros((2, UNITS[SHIFT][1], cells), far.dtype)
    for side, n in (("low", 0), ("high", 1)):
        @pl.when(jnp.logical_not(has[side]))
        def _(n=n):
            halo[n] = jnp.zeros(halo.shape[1:], halo.dtype)

    def widen(source, target, row):
        def body(k, carry):
            lane = pl.ds(pl.multiple_of(k * 128, 128), 128)
            target[:, :, k] = source[:, :, row, lane].astype(jnp.float32)
            return carry

        lax.fori_loop(0, cells // 128, body, 0, unroll=2)

    def add_up(base, far_base, height, groups, output=None):
        pairs = height // 2
        first = PLACE.get(groups[0][0][0])
        count = sum(2 * len(edges) + len(dates) for edges, dates in groups)
        needed = sorted({b for edges, _ in groups for a, m in edges for b in (a, a + m)})

        def body(k, total):
            packed = []
            weights = []
            for part in range(LANES // 128):
                tile = k * (LANES // 128) + part
                value = {}
                for a in needed:
                    value[a] = []
                    for c in range(2):
                        for odd in range(2):
                            row = pl.ds((base if 4 <= a < 8 else far_base) + odd, pairs, stride=2)
                            if 4 <= a < 8:
                                value[a].append(own_wide[c, a - 4, tile, row])
                            elif a == 1:
                                value[a].append(extra_wide[c, 0, tile, row])
                            elif a < 4:
                                value[a].append(far_wide[0, c, a - 2, tile, row])
                            else:
                                value[a].append(far_wide[1, c, a - 8, tile, row])
                terms = []
                for pairs_of, alone in groups:
                    for a, m in pairs_of:
                        (x, z, y, w), (u, p, v, q) = value[a], value[a + m]
                        terms.append((x * u + y * v) + (z * p + w * q))
                        terms.append((y * u - x * v) + (w * p - z * q))
                    for a in alone:
                        x, z, y, w = value[a]
                        terms.append((x * x + y * y) + (z * z + w * w))
                left = jnp.concatenate(terms, axis=0)
                high = left.astype(jnp.bfloat16)
                low = (left - high.astype(jnp.float32)).astype(jnp.bfloat16)
                packed += [high, low]
                weights.append(sel[tile])
            left = jnp.concatenate(packed, axis=1)
            right = jnp.concatenate(weights, axis=0)
            return total + jnp.dot(left, right, preferred_element_type=jnp.float32)

        total = lax.fori_loop(0, cells // LANES, body, jnp.zeros((count * pairs, columns), jnp.float32))
        total = total.reshape(count, pairs, columns)
        if output is None:
            sums[pl.ds(first, count), pl.ds(PAD + base // 2, pairs), :] = total
        else:
            output[pl.ds(0, count)] = total

    def windows(q, block):
        base = PAD + block * BLOCK * 2

        def every(shift):
            return sums[q, pl.ds(base + shift, BLOCK, stride=2), :]

        inner = every(0) + every(1)
        return inner, inner + (every(-1) + every(2))

    def finish(block, edges, power):
        for a, m in edges:
            for b in (a, a + m):
                if b not in power:
                    power[b] = windows(POWER[b], block)[1]
            look_re, win_re = windows(PLACE[a, m], block)
            look_im, win_im = windows(PLACE[a, m] + 1, block)
            size = jnp.sqrt(win_re * win_re + win_im * win_im)
            part = pl.ds(block * BLOCK, BLOCK)
            results[slot(a, m), 0, part] = look_re * (1.0 / (LOOK_AZ * LOOK_RG))
            results[slot(a, m), 1, part] = look_im * (1.0 / (LOOK_AZ * LOOK_RG))
            results[slot(a, m), 2, part] = size / jnp.sqrt(power[a] * power[a + m] + EPS)

    for step in range(rows // INNER_ROWS):
        own_copy(step).wait()
        row = pl.ds(step * INNER_ROWS, INNER_ROWS)
        widen(own, own_wide.at[:, :, :, row], row)
        add_up(step * INNER_ROWS, 0, INNER_ROWS, GROUPS["inner"])

    @pl.when(greets["high"] & later["high"])
    def _():
        pl.semaphore_wait(barrier, 1)

    def on_strip(which, body):
        for side, n in (("high", 0), ("low", 1)):
            @pl.when(has[side] & remote[side] & which)
            def _(side=side, n=n):
                body(side, n)

    def send_edges():
        for q in range(N_ALL):
            edge_sums[0, pl.ds(q, 1)] = sums[q, pl.ds(PAD + rows // 2 - 1, 1)]
            edge_sums[1, pl.ds(q, 1)] = sums[q, pl.ds(PAD, 1)]
        for side, n in (("high", 0), ("low", 1)):
            @pl.when(has[side] & jnp.logical_not(remote[side]))
            def _(side=side, n=n):
                halo_copy(n, edge_sums.at[n], side, halo_send.at[n]).start()
        on_strip(inner, lambda side, n: halo_copy(n, edge_sums.at[n], side, halo_send.at[n]).start())
        for at, toward in ((0, "next"), (3, "prev")):
            on_strip(place == at, lambda side, n, toward=toward: relay_out(n, toward).start())

    def relay_out(n, toward):
        return halo_copy(n, edge_sums.at[n], toward, relay_send.at[0], relayed.at[0], relay_recv.at[0])

    def relay_over(side, n):
        return halo_copy(n, relayed.at[0], side, relay_send.at[1], relayed.at[1], relay_recv.at[1])

    def relay_back(n, toward):
        return halo_copy(1 - n, relayed.at[1], toward, relay_send.at[2])

    def pass_over(side, n):
        relay_out(n, "next").wait_recv()
        relay_over(side, n).start()

    def pass_back():
        for at, toward in ((1, "prev"), (2, "next")):
            def body(side, n, toward=toward):
                relay_over(side, n).wait_recv()
                relay_back(n, toward).start()
            on_strip(place == at, body)

    def take_halo():
        for side, opposite, n in (("low", "high", 0), ("high", "low", 1)):
            @pl.when(has[side])
            def _(opposite=opposite, n=n):
                halo_copy(n, edge_sums.at[n], opposite, halo_send.at[n]).wait_recv()
        for q in range(N_ALL):
            sums[q, pl.ds(PAD - 1, 1)] = halo[0, pl.ds(q, 1)]
            sums[q, pl.ds(PAD + rows // 2, 1)] = halo[1, pl.ds(q, 1)]

    def finish_block(name, block):
        power = {}
        edges = edges_of(name)
        for side in ("next", "prev"):
            owed = [edge for edge in edges if ships(side, edge, block)]
            finish(block, owed, power)
            if owed:
                @pl.when(has[side])
                def _(side=side, owed=owed):
                    for edge in owed:
                        ship_copy(side, edge, block).start()
        done = SHIPPED["next"] + SHIPPED["prev"]
        finish(block, [edge for edge in edges if edge not in done], power)

    def lend():
        first, height, _ = UNITS[SHIFT]
        extra_copy().wait_recv()
        widen(extra, extra_wide, pl.ds(0, height))
        add_up(first, 0, height, [([(1, 4)], [])], lent)
        row = pl.ds(PAD + first // 2, height // 2)
        for i, edge in enumerate(((2, 3), (3, 2))):
            lent[pl.ds(2 + 2 * i, 2)] = sums[pl.ds(PLACE[edge], 2), row]
        lent[6] = sums[POWER[5], row]
        lend_copy().start()

    def borrow():
        first, height, _ = UNITS[SHIFT]
        lend_copy().wait_recv()
        row = pl.ds(PAD + first // 2, height // 2)
        for i, edge in enumerate(((5, 4), (6, 3), (7, 2))):
            sums[pl.ds(PLACE[edge], 2), row] = borrowed[pl.ds(2 * i, 2)]
        sums[POWER[9], row] = borrowed[6]

    ready = {"inner": set(range(rows)), NEAR: set(), OTHER: set()}
    finished = set()
    for unit, (first, height, dates) in enumerate(UNITS):
        for side in ("prev", "next") if unit < LAST else ():
            @pl.when(comes(side, unit))
            def _(side=side):
                image_copy("next" if side == "prev" else "prev", unit).wait_recv()
        for device in range(2):
            ahead = IN_FLIGHT[0 if unit >= CATCH_UP else device]
            while started[device] < min(unit + 1 + ahead, len(UNITS)):
                send(started[device], device)
                started[device] += 1
        if unit == HALO_AT:
            take_halo()
        if unit == BORROW_AT:
            pl.when(late)(borrow)
            ready[OTHER] |= set(range(UNITS[SHIFT][0], UNITS[SHIFT][0] + UNITS[SHIFT][1]))
        def widen_side(side):
            low, high = dates if side else (2 - dates[1], 2 - dates[0])
            date = pl.ds(low, high - low)
            widen(far.at[side, :, date], far_wide.at[side, :, date, :, pl.ds(0, height)], pl.ds(first, height))

        for side in range(2) if unit < LAST else ():
            widen_side(side)
        names = [name for name in (NEAR, OTHER) if dates[0] <= name[0] and name[1] <= dates[1]]
        if unit == LAST:
            for n, (side, source) in enumerate((("next", "prev"), ("prev", "next"))):
                @pl.when(has[side])
                def _(source=source):
                    image_copy(source, unit).wait_recv()
                widen_side(1 - n)
                add_up(first, 0, height, GROUPS[OTHER][n : n + 1])
                for block in range(TAIL_BLOCKS):
                    finish(block, [TAIL[side]], {})
                @pl.when(has[side])
                def _(side=side):
                    tail_copy(side).start()
            add_up(first, 0, height, GROUPS[OTHER][2:])
        else:
            add_up(first, 0, height, [group for name in names for group in GROUPS[name]])
        for name in names:
            if unit != SHIFT:
                ready[name] |= set(range(first, first + height))
        if unit == SHIFT:
            pl.when(early)(lend)
        if unit == EDGES_AT:
            send_edges()
        if unit == RELAY_AT[0]:
            on_strip(inner, pass_over)
        if unit == RELAY_AT[1]:
            pass_back()
        if unit > EDGES_AT:
            for name in (NEAR, OTHER, "inner"):
                for block in range(blocks):
                    height_of = BLOCK * LOOK_AZ
                    reach = set(range(max(block * height_of - 2, 0), min((block + 1) * height_of + 2, rows)))
                    inside = 0 < block < blocks - 1
                    least = (0 if inside else LAST) if name == "inner" else (SHIP_AT if inside else HALO_AT)
                    if (name, block) not in finished and reach <= ready[name] and unit >= least:
                        finish_block(name, block)
                        finished.add((name, block))

    for side, opposite in (("next", "prev"), ("prev", "next")):
        @pl.when(has[side])
        def _(side=side, opposite=opposite):
            for block in range(blocks):
                for edge in SHIPPED[opposite]:
                    if ships(opposite, edge, block):
                        ship_copy(opposite, edge, block).wait_recv()

    offset_copy.wait()
    places = {}
    for i in range(OWN):
        for k in range(4):
            offset = offsets[i, k]
            place = 4 * (OWN + i + jnp.minimum(offset, 0)) + jnp.abs(offset) - 1
            sign = jnp.where(offset > 0, 1.0, -1.0)
            places[i, k] = place
            chosen = results[place]
            interferogram[i, k, 0] = chosen[0]
            interferogram[i, k, 1] = chosen[1] * sign
            coherence[i, k] = chosen[2]

    for n, side, i, sign in ((0, "prev", 1, -1.0), (1, "next", 2, 1.0)):
        @pl.when(has[side])
        def _(side=side):
            tail_copy("next" if side == "prev" else "prev").wait_recv()
        part = pl.ds(0, TAIL_BLOCKS * BLOCK)
        for k in range(4):
            here = places[i, k] == (7, 27)[n]
            interferogram[i, k, 0, part] = jnp.where(here, tail[n, 0], interferogram[i, k, 0, part])
            interferogram[i, k, 1, part] = jnp.where(here, tail[n, 1] * sign, interferogram[i, k, 1, part])
            coherence[i, k, part] = jnp.where(here, tail[n, 2], coherence[i, k, part])

    for side in ("next", "prev"):
        @pl.when(has[side])
        def _(side=side):
            for unit in range(len(UNITS)):
                if (side, unit) != ("prev", SHIFT):
                    image_copy(side, unit).wait_send()
            tail_copy(side).wait_send()
            for block in range(blocks):
                for edge in SHIPPED[side]:
                    if ships(side, edge, block):
                        ship_copy(side, edge, block).wait_send()
    @pl.when(goes("prev", SHIFT))
    def _():
        image_copy("prev", SHIFT).wait_send()
    @pl.when(late)
    def _():
        extra_copy().wait_send()
    @pl.when(early)
    def _():
        lend_copy().wait_send()
    for side, n in (("high", 0), ("low", 1)):
        @pl.when(has[side] & (inner | jnp.logical_not(remote[side])))
        def _(side=side, n=n):
            halo_copy(n, edge_sums.at[n], side, halo_send.at[n]).wait_send()
    on_strip(jnp.logical_not(inner), lambda side, n: relay_out(n, "next").wait_send())
    on_strip(inner, lambda side, n: relay_over(side, n).wait_send())
    on_strip(inner, lambda side, n: relay_back(n, "next").wait_send())


def per_device(slc, partner_offset):
    _, dates, rows, cells = slc.shape
    columns = cells // LOOK_RG
    looks = rows // LOOK_AZ
    steps = rows // INNER_ROWS
    blocks = looks // BLOCK
    f32 = jnp.float32
    return pl.pallas_call(
        kernel,
        out_shape=(
            jax.ShapeDtypeStruct((dates, 4, 2, looks, columns), f32),
            jax.ShapeDtypeStruct((dates, 4, looks, columns), f32),
        ),
        in_specs=[
            pl.BlockSpec(memory_space=pltpu.HBM),
            pl.BlockSpec(memory_space=pltpu.HBM),
        ],
        out_specs=[pl.BlockSpec(memory_space=pltpu.VMEM)] * 2,
        scratch_shapes=[
            pltpu.SMEM(partner_offset.shape, partner_offset.dtype),
            pltpu.VMEM((2, dates, rows, cells), slc.dtype),
            pltpu.VMEM((2, 2, 2, rows, cells), slc.dtype),
            pltpu.VMEM((2, dates, cells // 128, rows, 128), f32),
            pltpu.VMEM((2, 2, 2, cells // 128, INNER_ROWS, 128), f32),
            pltpu.VMEM((cells // 128, 256, columns), jnp.bfloat16),
            pltpu.VMEM((N_ALL, rows // 2 + 2 * PAD, columns), f32),
            pltpu.VMEM((2, N_ALL, columns), f32),
            pltpu.VMEM((2, N_ALL, columns), f32),
            pltpu.VMEM((2, N_ALL, columns), f32),
            pltpu.VMEM((32, 3, looks, columns), f32),
            pltpu.VMEM((2, 3, TAIL_BLOCKS * BLOCK, columns), f32),
            pltpu.VMEM((2, 1, UNITS[SHIFT][1], cells), slc.dtype),
            pltpu.VMEM((2, 1, cells // 128, UNITS[SHIFT][1], 128), f32),
            pltpu.VMEM((7, UNITS[SHIFT][1] // 2, columns), f32),
            pltpu.VMEM((7, UNITS[SHIFT][1] // 2, columns), f32),
            pltpu.SemaphoreType.DMA,
            pltpu.SemaphoreType.DMA((steps,)),
            pltpu.SemaphoreType.DMA((2, len(UNITS))),
            pltpu.SemaphoreType.DMA((2, len(UNITS))),
            pltpu.SemaphoreType.DMA((2,)),
            pltpu.SemaphoreType.DMA((2,)),
            pltpu.SemaphoreType.DMA((3,)),
            pltpu.SemaphoreType.DMA((2,)),
            pltpu.SemaphoreType.DMA((2, 3, blocks)),
            pltpu.SemaphoreType.DMA((2, 3, blocks)),
            pltpu.SemaphoreType.DMA((2,)),
            pltpu.SemaphoreType.DMA((2,)),
            pltpu.SemaphoreType.DMA((2,)),
            pltpu.SemaphoreType.DMA((2,)),
        ],
        compiler_params=pltpu.CompilerParams(
            collective_id=0, has_side_effects=True, vmem_limit_bytes=211 * 1024 * 256
        ),
    )(partner_offset, slc)


def solution(mesh):
    return jax.shard_map(
        per_device,
        mesh=mesh,
        in_specs=(P(None, "date", "strip", None), P("date", None)),
        out_specs=(P("date", None, None, "strip", None), P("date", None, "strip", None)),
        check_vma=False,
    )
```
